128 devices in a mesh: wide: 32 (over z, y, core), narrow: 4 (over x).
Axes of the slice: x: 4, y: 4, z: 4, core: 2. Of those that a mesh axis runs over, the one named last changes fastest.
Arguments:
- desc_a: bfloat16 [16384, 128], P('wide'), may hold values from -6 to 6
- desc_b: bfloat16 [32768, 128], P('narrow'), may hold values from -6 to 6
- logmass_a: float32 [16384], P('wide'), may hold values from -6 to 6
- logmass_b: float32 [32768], P('narrow'), may hold values from -6 to 6
- g_start: float32 [32768], P('narrow'), may hold values from -1 to 16, as said below
Outputs:
- potential_a: float32 [16384], P('wide')
- potential_b: float32 [32768], P('narrow')
- flow_a: float32 [16384, 128], P('wide')
- flow_b: float32 [32768, 128], P(('narrow', 'wide'))
The draws below stay inside these ranges and needn't reach their ends.
Inputs may be any that keep to these rules, and one draw needn't show every extreme that they name: `g_start`: potentials of view B carried over from the previous pair of views.
All inputs are finite; a program needn't handle non-finite values.
Results may differ from the reference program's by a relative error of at most 0.01.
Values may be sent and summed in bfloat16 or wider, within the bound.
No kernel may reach another device: no remote copies, remote signals or barrier semaphores. Data moves between devices by JAX's collectives and lax.ppermute only.
A program may use at most 64 MiB of HBM per device.

```python
import math
import jax
import jax.numpy as jnp
from jax import lax

DIM = 128
ITERS = 2
NA = 16384
NB = 32768


def draw_g_start(key, part):
    third_key = jax.random.fold_in(key, 2)
    values = 0.3 * jax.random.normal(third_key, (NB,), jnp.float32)
    return jnp.clip(values, -1.0, 1.0)


def level_of(key, dims, shards, low, high):
    loudness = 1.0
    for position, parts in shards:
        draws = jax.random.uniform(jax.random.fold_in(jax.random.fold_in(key, 6), position), (parts,), jnp.float32, low / len(shards), high / len(shards))
        loudness = loudness * jnp.repeat(jnp.exp(draws), dims[position] // parts).reshape((-1,) + (1,) * (len(dims) - 1 - position))
    return loudness


def gaussian(stream_key, dims, width, most, cuts=(), dtype=jnp.bfloat16):
    factor_of = level_of(stream_key, dims, cuts, -0.22, 0.18) if cuts else 1.0
    values = jax.random.normal(stream_key, dims, jnp.float32) * width * factor_of
    return jnp.minimum(jnp.maximum(values, -most), most).astype(dtype)


def setup_inputs(seed: int = 0) -> dict:
    arg_keys = jax.random.split(jax.random.key(seed), 6)
    desc_a = gaussian(arg_keys[0], (NA, DIM), 1.0, 6.0, ((0, 32),))
    desc_b = gaussian(arg_keys[1], (NB, DIM), 1.0, 6.0, ((0, 4),))
    logmass_a = gaussian(arg_keys[2], (NA,), 2.0, 6.0, ((0, 32),), jnp.float32)
    logmass_b = gaussian(arg_keys[3], (NB,), 2.0, 6.0, ((0, 4),), jnp.float32)
    g_start = draw_g_start(jax.random.fold_in(arg_keys[5], 71), 0)
    return dict(desc_a=desc_a, desc_b=desc_b, logmass_a=logmass_a, logmass_b=logmass_b, g_start=g_start)


EPS = 0.05

def unit_rows(desc):
    wide32 = desc.astype(jnp.float32)
    return (wide32 / jnp.sqrt(lax.optimization_barrier(jnp.sum(wide32 * wide32, axis=1, keepdims=True)) + 1e-06)).astype(jnp.bfloat16)

def cost_of(left, right):
    return 2.0 - 2.0 * jnp.dot(left, right.T, preferred_element_type=jnp.float32)

def reference(desc_a, desc_b, logmass_a, logmass_b, g_start):
    unit_a = unit_rows(desc_a)
    unit_b = unit_rows(desc_b)
    n_tokens = unit_a.shape[0]
    feat_width = unit_a.shape[1]
    row_step = math.gcd(n_tokens, 512)
    a_tiles = unit_a.reshape(-1, row_step, feat_width)

    def row_lse(potential):

        def one_tile(tile_a):
            scores = (potential[None, :] - cost_of(tile_a, unit_b)) / EPS
            highest = lax.optimization_barrier(jnp.max(scores, axis=1))
            return highest + jnp.log(lax.optimization_barrier(jnp.sum(jnp.exp(scores - highest[:, None]), axis=1)))
        return lax.map(one_tile, a_tiles).reshape(-1)

    def col_lse(row_pot):

        def one_tile(state_now, inputs):
            highest, summed = state_now
            tile_a, row_part = inputs
            scores = (row_part[:, None] - cost_of(tile_a, unit_b)) / EPS
            new_high = jnp.maximum(highest, lax.optimization_barrier(jnp.max(scores, axis=0)))
            summed = summed * jnp.exp(highest - new_high) + lax.optimization_barrier(jnp.sum(jnp.exp(scores - new_high[None, :]), axis=0))
            return ((new_high, summed), None)
        init = (jnp.full((unit_b.shape[0],), -jnp.inf, jnp.float32), jnp.zeros((unit_b.shape[0],), jnp.float32))
        (highest, summed), _ = lax.scan(one_tile, init, (a_tiles, row_pot.reshape(-1, row_step)))
        return highest + jnp.log(summed)
    potential_b = g_start
    for sweep_index in range(ITERS):
        row_pot = EPS * logmass_a - EPS * row_lse(potential_b)
        lse_b = col_lse(row_pot)
        potential_b = EPS * logmass_b - EPS * lse_b

    def add_flow(state_now, inputs):
        tile_a, row_part = inputs
        weights = jnp.exp((row_part[:, None] - cost_of(tile_a, unit_b)) / EPS - lse_b[None, :]).astype(jnp.bfloat16)
        return (state_now + jnp.dot(weights.T, tile_a, preferred_element_type=jnp.float32), None)
    sums_b, _ = lax.scan(add_flow, jnp.zeros((unit_b.shape[0], feat_width), jnp.float32), (a_tiles, row_pot.reshape(-1, row_step)))
    flow_b = sums_b - unit_b.astype(jnp.float32)
    lse_a = row_lse(potential_b)
    potential_a = EPS * logmass_a - EPS * lse_a

    def flow_tile(inputs):
        tile_a, lse_part = inputs
        weights = jnp.exp((potential_b[None, :] - cost_of(tile_a, unit_b)) / EPS - lse_part[:, None]).astype(jnp.bfloat16)
        return jnp.dot(weights, unit_b, preferred_element_type=jnp.float32) - tile_a.astype(jnp.float32)
    flow_a = lax.map(flow_tile, (a_tiles, lse_a.reshape(-1, row_step))).reshape(n_tokens, feat_width)
    return (potential_a, potential_b, flow_a, flow_b)
```

```python
import functools
import math

import jax
import jax.numpy as jnp
from jax import lax
from jax.experimental import pallas as pl
from jax.experimental.pallas import tpu as pltpu
from jax.sharding import Mesh, PartitionSpec as P

EPS = 0.05
LOG2E = math.log2(math.e)
C2 = LOG2E / EPS
TOP = 50.0
DIM = 128
F32 = jnp.float32
BF16 = jnp.bfloat16


NR = 1024
NC = 4096
CH = 256
NK = NC // CH
NPEER = 8
NZY = 16


def nt(left, right):
    return lax.dot_general(left, right, (((1,), (1,)), ((), ())), preferred_element_type=F32)


def nn(left, right):
    return lax.dot_general(left, right, (((1,), (0,)), ((), ())), preferred_element_type=F32)


def split_rows(vec, rows_ref):
    high = vec.astype(BF16).astype(F32)
    low = vec - high
    for r in range(vec.shape[0]):
        rows_ref[0:1, r * 128 : (r + 1) * 128] = high[r : r + 1, :]
        rows_ref[1:2, r * 128 : (r + 1) * 128] = low[r : r + 1, :]


def combine(parts_ref, count, rows):
    shifts = [parts_ref[d, rows : rows + 8, :] for d in range(count)]
    top = functools.reduce(jnp.maximum, shifts)
    total = None
    for d in range(count):
        half = jnp.exp2(0.5 * (shifts[d][0:1, :] - top[0:1, :]))
        term = parts_ref[d, 0:rows, :] * half * half
        total = term if total is None else total + term
    return total, top


def pick_cols(ref, core, out_ref):
    for k in range(NK):
        first = ref[4 * k : 4 * k + 2, :]
        second = ref[4 * k + 2 : 4 * k + 4, :]
        out_ref[2 * k : 2 * k + 2, :] = jnp.where(core == 0, first, second)


def send_all(msg_ref, count, sums, shift):
    rows = sums.shape[0]
    for d in range(count):
        msg_ref[d, 0:rows, :] = sums
        msg_ref[d, rows : rows + 8, :] = jnp.broadcast_to(shift, (8, 128))


def unit_t(raw):
    norm = jnp.sqrt(jnp.sum(raw * raw, axis=0, keepdims=True) + 1e-06)
    return (raw / norm).astype(BF16)


def first_kernel(place, desc_a, other_a, desc_b, g_all, lb_all,
                 k_out, at_out, bt_out, lb_out, msg,
                 a_unit, b_raw, vec, rows, acc, sems):
    core = place[0]
    for k in range(NK):
        pltpu.make_async_copy(desc_b.at[k, core], b_raw.at[k], sems.at[k]).start()
    for half, src in ((core, desc_a), (1 - core, other_a)):
        for m in range(2):
            raw_t = src[m * 256 : (m + 1) * 256, :].astype(F32).T
            unit = unit_t(raw_t)
            at = pl.multiple_of(half * 512 + m * 256, 256)
            at_out[:, pl.ds(at, 256)] = unit
            a_unit[pl.ds(at, 256), :] = unit.astype(F32).T.astype(BF16)
    pick_cols(lb_all, core, lb_out)
    pick_cols(g_all, core, vec)
    pot = vec[...] * C2
    shift = jnp.max(jnp.max(pot, axis=0, keepdims=True), axis=1, keepdims=True)
    rows[...] = jnp.zeros_like(rows)
    split_rows(jnp.exp2(pot - shift + TOP), rows)
    acc[...] = jnp.zeros_like(acc)

    def chunk(k, carry):
        pltpu.make_async_copy(desc_b.at[k, core], b_raw.at[k], sems.at[k]).wait()
        at = pl.multiple_of(k * CH, CH)
        bt = unit_t(b_raw[k].astype(F32).T)
        bt_out[:, pl.ds(at, CH)] = bt
        lhs = rows[:, pl.ds(at, CH)].astype(BF16)
        for m in range(NR // 256):
            span = slice(m * 256, (m + 1) * 256)
            cos = nn(a_unit[span, :], bt)
            kb = jnp.exp2(cos * (2.0 * C2)).astype(BF16)
            k_out[span, pl.ds(at, CH)] = kb
            acc[:, span] += nt(lhs, kb)
        return carry

    lax.fori_loop(0, NK, chunk, 0)
    sums = jnp.concatenate(
        [acc[0:1, r * 128 : (r + 1) * 128] + acc[1:2, r * 128 : (r + 1) * 128] for r in range(8)], axis=0
    )
    send_all(msg, NPEER, sums, shift)


def row_scales(parts, la, rows):
    total, top = combine(parts, NPEER, 8)
    level = la[...] * LOG2E - jnp.log2(total)
    shift = jnp.max(jnp.max(level, axis=0, keepdims=True), axis=1, keepdims=True)
    rows[...] = jnp.zeros_like(rows)
    split_rows(jnp.exp2(level - shift + TOP), rows)
    return shift, top


def col_kernel(parts, la, k_mat, base, msg, base_out, rows, vec):
    shift, top = row_scales(parts, la, rows)
    base_out[...] = base[...] + top

    def chunk(k, carry):
        at = pl.multiple_of(k * 512, 512)
        part = nn(rows[...].astype(BF16), k_mat[:, pl.ds(at, 512)])
        part = part[0:1, :] + part[1:2, :]
        for r in range(4):
            vec[pl.ds(k * 4 + r, 1), :] = part[:, r * 128 : (r + 1) * 128]
        return carry

    lax.fori_loop(0, NC // 512, chunk, 0)
    send_all(msg, NZY, vec[...], shift)


def col_flow_kernel(parts, la, k_mat, base, a_t, msg, sums_out, base_out, rows, vec, lhs):
    shift, top = row_scales(parts, la, rows)
    base_out[...] = base[...] + top
    scale = rows[0:1, :] + rows[1:2, :]
    lhs[0:128, :] = (a_t[...].astype(F32) * scale).astype(BF16)
    lhs[128:144, :] = rows[...].astype(BF16)

    def chunk(k, carry):
        at = pl.multiple_of(k * CH, CH)
        part = nn(lhs[...], k_mat[:, pl.ds(at, CH)])
        sums_out[k] = part[0:128, :].astype(BF16)
        total = part[128:129, :] + part[129:130, :]
        for r in range(2):
            vec[pl.ds(k * 2 + r, 1), :] = total[:, r * 128 : (r + 1) * 128]
        return carry

    lax.fori_loop(0, NK, chunk, 0)
    send_all(msg, NZY, vec[...], shift)


def col_scales(parts, lb, rows):
    total, top = combine(parts, NZY, 32)
    log_total = jnp.log2(total)
    level = lb[...] * LOG2E - log_total
    shift = jnp.max(jnp.max(level, axis=0, keepdims=True), axis=1, keepdims=True)
    shift = jnp.ceil(shift)
    rows[...] = jnp.zeros_like(rows)
    split_rows(jnp.exp2(level - shift + TOP), rows)
    return level, total, shift, top


def row_kernel(parts, lb, k_mat, base, msg, base_out, rows, acc):
    level, total, shift, top = col_scales(parts, lb, rows)
    base_out[...] = base[...] - top
    acc[...] = jnp.zeros_like(acc)

    def chunk(k, carry):
        at = pl.multiple_of(k * 512, 512)
        lhs = rows[:, pl.ds(at, 512)].astype(BF16)
        acc[...] += nt(lhs, k_mat[:, pl.ds(at, 512)])
        return carry

    lax.fori_loop(0, NC // 512, chunk, 0)
    sums = jnp.concatenate(
        [acc[0:1, r * 128 : (r + 1) * 128] + acc[1:2, r * 128 : (r + 1) * 128] for r in range(8)], axis=0
    )
    send_all(msg, NPEER, sums, shift)


def pack_rows(out_ref, flow, total, shift):
    n = flow.shape[1]
    out_ref[0:128, :] = flow.astype(BF16)
    high = total.astype(BF16).astype(F32)
    kind = lax.broadcasted_iota(jnp.int32, (16, n), 0)
    tail = jnp.where(kind == 0, high, jnp.where(kind == 1, total - high, jnp.where(kind == 2, shift, 0.0)))
    out_ref[128:144, :] = tail.astype(BF16)


def row_flow_kernel(place, parts, lb, k_mat, base, b_t, own_out, other_out, pot_out, total_out, base_out, rows, lhs, acc):
    core = place[0]
    level, total, shift, top = col_scales(parts, lb, rows)
    level_base = base[...] - top
    base_out[...] = level_base
    pot_out[...] = (level + level_base[0:1, :]) * (1.0 / C2)
    total_out[...] = total
    scale = rows[0:1, :] + rows[1:2, :]
    lhs[0:128, :] = (b_t[...].astype(F32) * scale).astype(BF16)
    lhs[128:144, :] = rows[...].astype(BF16)
    acc[...] = jnp.zeros_like(acc)

    def chunk(k, carry):
        at = pl.multiple_of(k * 512, 512)
        acc[...] += nt(lhs[:, pl.ds(at, 512)], k_mat[:, pl.ds(at, 512)])
        return carry

    lax.fori_loop(0, NC // 512, chunk, 0)
    for half, out in ((core, own_out), (1 - core, other_out)):
        part = acc[:, pl.ds(pl.multiple_of(half * 512, 512), 512)]
        pack_rows(out, part[0:128, :], part[128:129, :] + part[129:130, :], shift)


def pair_sum(terms):
    while len(terms) > 1:
        terms = [terms[i] + terms[i + 1] for i in range(0, len(terms), 2)]
    return terms[0]


def merge(parts):
    tails = [p[128:144, :].astype(F32) for p in parts]
    shifts = [t[2:3, :] for t in tails]
    top = functools.reduce(jnp.maximum, shifts)
    flows, totals = [], []
    for p, t, s in zip(parts, tails, shifts):
        half = jnp.exp2(0.5 * (s - top))
        flows.append(p[0:128, :].astype(F32) * half * half)
        totals.append((t[0:1, :] + t[1:2, :]) * half * half)
    return pair_sum(flows), pair_sum(totals), top


def merge_kernel(own, received, out):
    flow, total, top = merge([own, received])
    pack_rows(out, flow, total, top)


def final_a_kernel(p0, p1, p2, p3, desc_a, la, base, flow_out, pot_out):
    flow, total, top = merge([p0, p2, p1, p3])
    flow_t = flow / total
    level = jnp.log2(total) + (top - TOP - 2.0 * C2)
    for r in range(4):
        here = slice(r * 128, (r + 1) * 128)
        unit = unit_t(desc_a[here, :].astype(F32).T).astype(F32)
        flow_out[here, :] = (flow_t[:, here] - unit).T
        pot_out[r : r + 1, :] = (la[r : r + 1, :] * LOG2E - level[:, here] - base[0:1, :]) * (1.0 / C2)


def final_b_kernel(place, sums, parts, total, b_t, own_pot, other_pot, flow_out, pot_out):
    core = place[0]
    chunk = place[1]
    shifts = [parts[d, 32:40, :] for d in range(NZY)]
    top = functools.reduce(jnp.maximum, shifts)
    acc = 0.0
    for d in range(NZY):
        half = jnp.exp2(0.5 * (shifts[d][0:1, 0:1] - top[0:1, 0:1]))
        acc = acc + sums[d].astype(F32) * half * half
    at = pl.multiple_of(chunk * CH, CH)
    unit = b_t[:, pl.ds(at, CH)].astype(F32)
    for r in range(2):
        here = slice(r * 128, (r + 1) * 128)
        denom = total[pl.ds(chunk * 2 + r, 1), :]
        flow_out[here, :] = (acc[:, here] / denom - unit[:, here]).T
    for k in range(NK):
        mine = own_pot[2 * k : 2 * k + 2, :]
        theirs = other_pot[2 * k : 2 * k + 2, :]
        pot_out[4 * k : 4 * k + 2, :] = jnp.where(core == 0, mine, theirs)
        pot_out[4 * k + 2 : 4 * k + 4, :] = jnp.where(core == 0, theirs, mine)


def sds(*shape, dtype=F32):
    return jax.ShapeDtypeStruct(shape, dtype)


VM = pl.BlockSpec(memory_space=pltpu.VMEM)
SM = pl.BlockSpec(memory_space=pltpu.SMEM)
ANY = pl.BlockSpec(memory_space=pl.ANY)


def call(kernel, ins, outs, scratch, flops=0, bytes_accessed=0, trans=0):
    return pl.pallas_call(
        kernel,
        in_specs=ins,
        out_specs=[VM] * len(outs),
        out_shape=outs,
        scratch_shapes=scratch,
        compiler_params=pltpu.CompilerParams(vmem_limit_bytes=40 * 1024 * 1024),
        cost_estimate=pl.CostEstimate(flops=flops, bytes_accessed=bytes_accessed, transcendentals=trans),
    )


PASS = NR * NC


def on_device(desc_a, desc_b, logmass_a, logmass_b, g_start):
    core = lax.axis_index("core")
    place = jnp.stack([core, lax.axis_index("zy")]).astype(jnp.int32)
    swap = [(0, 1), (1, 0)]
    la_own = logmass_a.reshape(4, 128)
    other_a = lax.ppermute(desc_a, "core", swap)
    la_other = lax.ppermute(la_own, "core", swap)
    la = jnp.where(
        core == 0,
        jnp.concatenate([la_own, la_other], axis=0),
        jnp.concatenate([la_other, la_own], axis=0),
    )
    k_mat, a_t, b_t, lb, msg = call(
        first_kernel,
        [SM, VM, VM, ANY, VM, VM],
        [pltpu.VMEM((NR, NC), BF16), sds(DIM, NR, dtype=BF16), sds(DIM, NC, dtype=BF16), sds(32, 128), sds(NPEER, 16, 128)],
        [
            pltpu.VMEM((NR, DIM), BF16),
            pltpu.VMEM((NK, CH, DIM), BF16),
            pltpu.VMEM((32, 128), F32),
            pltpu.VMEM((16, NC), F32),
            pltpu.VMEM((16, NR), F32),
            pltpu.SemaphoreType.DMA((NK,)),
        ],
        flops=2 * PASS * DIM,
        trans=PASS,
    )(place, desc_a, other_a, desc_b.reshape(NK, 2, CH, DIM), g_start.reshape(64, 128), logmass_b.reshape(64, 128))
    keep = lambda x: pltpu.with_memory_space_constraint(x, pltpu.VMEM)

    parts = lax.all_to_all(msg, ("core", "x"), 0, 0)
    base = jnp.zeros((8, 128), F32)
    msg, base = call(
        col_kernel,
        [VM] * 4,
        [sds(NZY, 40, 128), sds(8, 128)],
        [pltpu.VMEM((16, NR), F32), pltpu.VMEM((32, 128), F32)],
        flops=2 * PASS * 16,
    )(parts, la, keep(k_mat), base)

    parts = lax.all_to_all(msg, "zy", 0, 0)
    msg, base = call(
        row_kernel,
        [VM] * 4,
        [sds(NPEER, 16, 128), sds(8, 128)],
        [pltpu.VMEM((16, NC), F32), pltpu.VMEM((16, NR), F32)],
        flops=2 * PASS * 16,
    )(parts, lb, keep(k_mat), base)

    parts = lax.all_to_all(msg, ("core", "x"), 0, 0)
    msg, sums, base = call(
        col_flow_kernel,
        [VM] * 5,
        [sds(NZY, 40, 128), sds(NZY, DIM, CH, dtype=BF16), sds(8, 128)],
        [pltpu.VMEM((16, NR), F32), pltpu.VMEM((32, 128), F32), pltpu.VMEM((144, NR), BF16)],
        flops=2 * PASS * 144,
    )(parts, la, keep(k_mat), base, a_t)

    parts = lax.all_to_all(msg, "zy", 0, 0)
    sums = lax.all_to_all(sums, "zy", 0, 0)
    own, other, own_pot, total, base = call(
        row_flow_kernel,
        [SM] + [VM] * 5,
        [sds(144, 512, dtype=BF16), sds(144, 512, dtype=BF16), sds(32, 128), sds(32, 128), sds(8, 128)],
        [pltpu.VMEM((16, NC), F32), pltpu.VMEM((144, NC), BF16), pltpu.VMEM((144, NR), F32)],
        flops=2 * PASS * 144,
    )(place, parts, lb, keep(k_mat), base, b_t)

    received = lax.ppermute(other, "core", swap)
    other_pot = lax.ppermute(own_pot, "core", swap)
    mine = call(merge_kernel, [VM] * 2, [sds(144, 512, dtype=BF16)], [])(own, received)[0]
    others = [lax.ppermute(mine, "x", [(i, (i + s) % 4) for i in range(4)]) for s in (1, 2, 3)]
    flow_a, pot_a = call(
        final_a_kernel, [VM] * 7, [sds(512, DIM), sds(4, 128)], []
    )(mine, *others, desc_a, la_own, base)
    flow_b, pot_b = call(
        final_b_kernel, [SM] + [VM] * 6, [sds(CH, DIM), sds(64, 128)], []
    )(place, sums, parts, total, b_t, own_pot, other_pot)
    return (pot_a.reshape(512), pot_b.reshape(8192), flow_a, flow_b)


def solution(mesh):
    fine = Mesh(mesh.devices.reshape(NZY, 2, 4), ("zy", "core", "x"))
    wide = ("zy", "core")
    return jax.shard_map(
        on_device,
        mesh=fine,
        in_specs=(P(wide, None), P("x", None), P(wide), P("x"), P("x")),
        out_specs=(P(wide), P("x"), P(wide, None), P(("x", "zy", "core"), None)),
        check_vma=False,
    )
```

```python
import functools
import math

import jax
import jax.numpy as jnp
from jax import lax
from jax.experimental import pallas as pl
from jax.experimental.pallas import tpu as pltpu
from jax.sharding import Mesh, PartitionSpec as P

EPS = 0.05
LOG2E = math.log2(math.e)
C2 = LOG2E / EPS
TOP = 50.0
DIM = 128
F32 = jnp.float32
BF16 = jnp.bfloat16


NR = 1024
NC = 4096
CH = 256
NK = NC // CH
NPEER = 8
NZY = 16


def nt(left, right):
    return lax.dot_general(left, right, (((1,), (1,)), ((), ())), preferred_element_type=F32)


def nn(left, right):
    return lax.dot_general(left, right, (((1,), (0,)), ((), ())), preferred_element_type=F32)


def split_rows(vec, rows_ref):
    high = vec.astype(BF16).astype(F32)
    low = vec - high
    for r in range(vec.shape[0]):
        rows_ref[0:1, r * 128 : (r + 1) * 128] = high[r : r + 1, :]
        rows_ref[1:2, r * 128 : (r + 1) * 128] = low[r : r + 1, :]


def combine(parts_ref, count, rows):
    shifts = [parts_ref[d, rows : rows + 8, :] for d in range(count)]
    top = functools.reduce(jnp.maximum, shifts)
    total = None
    for d in range(count):
        half = jnp.exp2(0.5 * (shifts[d][0:1, :] - top[0:1, :]))
        term = parts_ref[d, 0:rows, :] * half * half
        total = term if total is None else total + term
    return total, top


def pair_sum(terms):
    while len(terms) > 1:
        terms = [terms[i] + terms[i + 1] for i in range(0, len(terms), 2)]
    return terms[0]


def pick_cols(ref, core, out_ref):
    for k in range(NK):
        first = ref[4 * k : 4 * k + 2, :]
        second = ref[4 * k + 2 : 4 * k + 4, :]
        out_ref[2 * k : 2 * k + 2, :] = jnp.where(core == 0, first, second)


def unit_t(raw):
    norm = jnp.sqrt(jnp.sum(raw * raw, axis=0, keepdims=True) + 1e-06)
    return (raw / norm).astype(BF16)


def prep_kernel(place, desc_b, g_all, lb_all, desc_a, a_out, b_out, bt_out, at_out, rows_out, shift_out, lb_out,
                b_raw, a_raw, g_raw, lb_raw, vec, rows, sems):
    core = place[0]
    copies = [
        pltpu.make_async_copy(g_all, g_raw, sems.at[NK]),
        pltpu.make_async_copy(desc_a, a_raw, sems.at[NK + 1]),
        pltpu.make_async_copy(lb_all, lb_raw, sems.at[NK + 2]),
    ]
    loads = [pltpu.make_async_copy(desc_b.at[k, core], b_raw.at[k], sems.at[k]) for k in range(NK)]
    for copy in copies + loads:
        copy.start()
    rows[...] = jnp.zeros_like(rows)
    for copy in copies:
        copy.wait()
    pick_cols(lb_raw, core, lb_out)
    pick_cols(g_raw, core, vec)
    pot = vec[...] * C2
    shift = jnp.max(jnp.max(pot, axis=0, keepdims=True), axis=1, keepdims=True)
    shift_out[...] = jnp.broadcast_to(shift, (8, 128))
    split_rows(jnp.exp2(pot - shift + TOP), rows)
    rows_out[...] = rows[...].astype(BF16)
    for m in range(2):
        span = slice(m * 256, (m + 1) * 256)
        unit = unit_t(a_raw[span, :].T.astype(F32))
        at_out[:, span] = unit
        a_out[span, :] = unit.T
    for k in range(NK):
        loads[k].wait()
        span = slice(k * CH, (k + 1) * CH)
        unit = unit_t(b_raw[k].T.astype(F32))
        bt_out[:, span] = unit
        b_out[span, :] = unit.T


def first_kernel(place, at_own, other_a, la_own, b_unit, rows, shift, kt_out, at_out, a_out, msg):
    core = place[0]
    for m in range(2):
        span = slice(m * 256, (m + 1) * 256)
        for half, unit in ((core, at_own[:, span]), (1 - core, unit_t(other_a[span, :].T.astype(F32)))):
            at = pl.multiple_of(half * 512 + m * 256, 256)
            at_out[:, pl.ds(at, 256)] = unit
            a_out[pl.ds(at, 256), :] = unit.T
    msg[16:20, :] = la_own[...]
    msg[20:24, :] = la_own[...]

    def block(j, carry):
        at = pl.multiple_of(j * 2048, 2048)
        for q in range(4):
            left = b_unit[pl.ds(at + q * 512, 512), :]
            for m in range(NR // 256):
                span = slice(m * 256, (m + 1) * 256)
                kt_out[pl.ds(at + q * 512, 512), span] = jnp.exp2(nn(left, at_out[:, span]) * (2.0 * C2)).astype(BF16)
        return carry

    lax.fori_loop(0, NC // 2048, block, 0)
    put_rows(msg, nn(rows[...], kt_out[...]), shift[0:1, :])


def put_rows(msg, part, shift):
    part = part[0:1, :] + part[1:2, :]
    for r in range(8):
        msg[r : r + 1, :] = part[:, r * 128 : (r + 1) * 128]
    msg[8:16, :] = jnp.broadcast_to(shift, (8, 128))


def merge_rows(parts):
    shifts = [p[8:16, :] for p in parts]
    top = functools.reduce(jnp.maximum, shifts)
    terms = []
    for part, shift in zip(parts, shifts):
        half = jnp.exp2(0.5 * (shift - top))
        terms.append(part[0:8, :] * half * half)
    return pair_sum(terms), top


def first_pair_kernel(place, own, received, out, la_out):
    pair_kernel(own, received, out)
    mine, theirs = own[16:20, :], received[16:20, :]
    la_out[0:4, :] = jnp.where(place[0] == 0, mine, theirs)
    la_out[4:8, :] = jnp.where(place[0] == 0, theirs, mine)


def pair_kernel(own, received, out):
    total, top = merge_rows([own, received])
    out[0:8, :] = total
    out[8:16, :] = top


def kernel_matrix(a_unit, b_t, k_out):
    def block(j, carry):
        at = pl.multiple_of(j * 512, 512)
        left = a_unit[pl.ds(at, 512), :]
        for m in range(NK):
            span = slice(m * CH, (m + 1) * CH)
            k_out[pl.ds(at, 512), span] = jnp.exp2(nn(left, b_t[:, span]) * (2.0 * C2)).astype(BF16)
        return carry

    lax.fori_loop(0, NR // 512, block, 0)


def row_scales(parts, la, rows):
    total, top = merge_rows(parts)
    level = la[...] * LOG2E - jnp.log2(total)
    shift = jnp.max(jnp.max(level, axis=0, keepdims=True), axis=1, keepdims=True)
    rows[...] = jnp.zeros_like(rows)
    scale = jnp.exp2(level - shift + TOP)
    split_rows(scale, rows)
    return scale, shift, top


def send_all(msg, shift):
    sums = msg[0, 0:32, :]
    for d in range(NZY):
        msg[d, 0:32, :] = sums
        msg[d, 32:40, :] = jnp.broadcast_to(shift, (8, 128))


def send_cols(msg, part, shift):
    part = part[0:1, :] + part[1:2, :]
    for r in range(32):
        msg[0, r : r + 1, :] = part[:, r * 128 : (r + 1) * 128]
    send_all(msg, shift)


def col_kernel(p0, p1, p2, p3, la, k_mat, msg, base_out, rows):
    scale, shift, top = row_scales([p0, p2, p1, p3], la, rows)
    base_out[...] = top
    send_cols(msg, nn(rows[...].astype(BF16), k_mat[...]), shift)


def last_col_kernel(p0, p1, p2, p3, la, k_mat, base, a_t, msg, sums_out, base_out, rows, lhs):
    scale, shift, top = row_scales([p0, p2, p1, p3], la, rows)
    base_out[...] = base[...] + top
    scale = rows[0:1, :] + rows[1:2, :]
    lhs[0:128, :] = (a_t[...].astype(F32) * scale).astype(BF16)
    lhs[128:144, :] = rows[...].astype(BF16)
    for k in range(NK):
        part = nn(lhs[...], k_mat[:, k * CH : (k + 1) * CH])
        sums_out[k] = part[0:128, :].astype(BF16)
        total = part[128:129, :] + part[129:130, :]
        msg[0, 2 * k : 2 * k + 1, :] = total[:, 0:128]
        msg[0, 2 * k + 1 : 2 * k + 2, :] = total[:, 128:256]
    send_all(msg, shift)


def col_scales(parts, lb, rows):
    total, top = combine(parts, NZY, 32)
    log_total = jnp.log2(total)
    level = lb[...] * LOG2E - log_total
    shift = jnp.max(jnp.max(level, axis=0, keepdims=True), axis=1, keepdims=True)
    shift = jnp.ceil(shift)
    rows[...] = jnp.zeros_like(rows)
    split_rows(jnp.exp2(level - shift + TOP), rows)
    return level, total, shift, top


def row_kernel(parts, lb, kt_mat, base, msg, base_out, rows):
    level, total, shift, top = col_scales(parts, lb, rows)
    base_out[...] = base[...] - top
    put_rows(msg, nn(rows[...].astype(BF16), kt_mat[...]), shift)


def pack_rows(out_ref, flow, total, shift):
    n = flow.shape[1]
    out_ref[0:128, :] = flow.astype(BF16)
    high = total.astype(BF16).astype(F32)
    kind = lax.broadcasted_iota(jnp.int32, (16, n), 0)
    tail = jnp.where(kind == 0, high, jnp.where(kind == 1, total - high, jnp.where(kind == 2, shift, 0.0)))
    out_ref[128:144, :] = tail.astype(BF16)


def row_flow_kernel(place, parts, lb, kt_mat, base, b_t, held, own_out, other_out, pot_out, total_out, base_out, held_out,
                    rows, lhs, acc):
    core = place[0]
    level, total, shift, top = col_scales(parts, lb, rows)
    level_base = base[...] - top
    base_out[...] = level_base
    pot_out[...] = (level + level_base[0:1, :]) * (1.0 / C2)
    total_out[...] = total
    scale = rows[0:1, :] + rows[1:2, :]
    lhs[0:128, :] = (b_t[...].astype(F32) * scale).astype(BF16)
    lhs[128:144, :] = rows[...].astype(BF16)
    acc[...] = nn(lhs[...], kt_mat[...])
    for half, out in ((core, own_out), (1 - core, other_out)):
        part = acc[:, pl.ds(pl.multiple_of(half * 512, 512), 512)]
        pack_rows(out, part[0:128, :], part[128:129, :] + part[129:130, :], shift)


def merge(parts):
    tails = [p[128:144, :].astype(F32) for p in parts]
    shifts = [t[2:3, :] for t in tails]
    top = functools.reduce(jnp.maximum, shifts)
    flows, totals = [], []
    for p, t, s in zip(parts, tails, shifts):
        half = jnp.exp2(0.5 * (s - top))
        flows.append(p[0:128, :].astype(F32) * half * half)
        totals.append((t[0:1, :] + t[1:2, :]) * half * half)
    return pair_sum(flows), pair_sum(totals), top


def merge_kernel(own, received, out):
    flow, total, top = merge([own, received])
    pack_rows(out, flow, total, top)


def final_a_kernel(p0, p1, p2, p3, a_own, la, base, flow_out, pot_out):
    flow, total, top = merge([p0, p2, p1, p3])
    flow_t = flow / total
    level = jnp.log2(total) + (top - TOP - 2.0 * C2)
    for r in range(4):
        here = slice(r * 128, (r + 1) * 128)
        flow_out[here, :] = flow_t[:, here].T - a_own[here, :].astype(F32)
        pot_out[r : r + 1, :] = (la[r : r + 1, :] * LOG2E - level[:, here] - base[0:1, :]) * (1.0 / C2)


def final_b_kernel(place, sums, parts, total, b_t, own_pot, other_pot, flow_out, pot_out):
    core = place[0]
    chunk = place[1]
    shifts = [parts[d, 32:40, :] for d in range(NZY)]
    top = functools.reduce(jnp.maximum, shifts)
    acc = 0.0
    for d in range(NZY):
        half = jnp.exp2(0.5 * (shifts[d][0:1, 0:1] - top[0:1, 0:1]))
        acc = acc + sums[d].astype(F32) * half * half
    at = pl.multiple_of(chunk * CH, CH)
    unit = b_t[:, pl.ds(at, CH)].astype(F32)
    for r in range(2):
        here = slice(r * 128, (r + 1) * 128)
        denom = total[pl.ds(chunk * 2 + r, 1), :]
        flow_out[here, :] = (acc[:, here] / denom - unit[:, here]).T
    for k in range(NK):
        mine = own_pot[2 * k : 2 * k + 2, :]
        theirs = other_pot[2 * k : 2 * k + 2, :]
        pot_out[4 * k : 4 * k + 2, :] = jnp.where(core == 0, mine, theirs)
        pot_out[4 * k + 2 : 4 * k + 4, :] = jnp.where(core == 0, theirs, mine)


def sds(*shape, dtype=F32):
    return jax.ShapeDtypeStruct(shape, dtype)


VM = pl.BlockSpec(memory_space=pltpu.VMEM)
SM = pl.BlockSpec(memory_space=pltpu.SMEM)
HB = pl.BlockSpec(memory_space=pltpu.HBM)
ANY = pl.BlockSpec(memory_space=pl.ANY)


def call(kernel, ins, outs, scratch=(), flops=0, bytes_accessed=0, trans=0, passes=None):
    return pl.pallas_call(
        kernel,
        in_specs=ins,
        out_specs=[ANY if i in (passes or {}).values() else VM for i in range(len(outs))],
        input_output_aliases=passes or {},
        out_shape=outs,
        scratch_shapes=list(scratch),
        compiler_params=pltpu.CompilerParams(vmem_limit_bytes=16 * 1024 * 1024),
        cost_estimate=pl.CostEstimate(flops=flops, bytes_accessed=bytes_accessed, transcendentals=trans),
    )


PASS = NR * NC


def on_device(desc_a, desc_b, logmass_a, logmass_b, g_start):
    core = lax.axis_index("core")
    place = jnp.stack([core, lax.axis_index("zy")]).astype(jnp.int32)
    swap = [(0, 1), (1, 0)]
    ring = [[(i, (i + s) % 4) for i in range(4)] for s in range(4)]
    keep = lambda x: pltpu.with_memory_space_constraint(x, pltpu.VMEM)
    stay = lambda x: pltpu.with_memory_space_constraint(x, pltpu.HBM)
    la_own = logmass_a.reshape(4, 128)
    other_a = lax.ppermute(desc_a, "core", swap)

    a_own, b_unit, b_t, at_own, rows, shift, lb = call(
        prep_kernel,
        [SM, HB, HB, HB, HB],
        [
            sds(512, DIM, dtype=BF16),
            sds(NC, DIM, dtype=BF16),
            sds(DIM, NC, dtype=BF16),
            sds(DIM, 512, dtype=BF16),
            sds(16, NC, dtype=BF16),
            sds(8, 128),
            sds(32, 128),
        ],
        [
            pltpu.VMEM((NK, CH, DIM), BF16),
            pltpu.VMEM((512, DIM), BF16),
            pltpu.VMEM((64, 128), F32),
            pltpu.VMEM((64, 128), F32),
            pltpu.VMEM((32, 128), F32),
            pltpu.VMEM((16, NC), F32),
            pltpu.SemaphoreType.DMA((NK + 3,)),
        ],
        flops=8 * NC * DIM,
        bytes_accessed=2 * NC * DIM,
    )(
        place,
        stay(desc_b.reshape(NK, 2, CH, DIM)),
        stay(g_start.reshape(64, 128)),
        stay(logmass_b.reshape(64, 128)),
        stay(desc_a),
    )


    kt_mat, a_t, a_unit, msg = call(
        first_kernel,
        [SM] + [VM] * 6,
        [pltpu.VMEM((NC, NR), BF16), sds(DIM, NR, dtype=BF16), sds(NR, DIM, dtype=BF16), sds(24, 128)],
        flops=2 * PASS * DIM,
        trans=PASS,
    )(place, at_own, other_a, la_own, b_unit, rows, shift)

    def over_x(pair):
        return [pair] + [lax.ppermute(pair, "x", ring[s]) for s in (1, 2, 3)]

    pair, la = call(first_pair_kernel, [SM] + [VM] * 2, [sds(16, 128), sds(8, 128)])(
        place, msg, lax.ppermute(msg, "core", swap)
    )
    k_mat = call(
        kernel_matrix, [VM] * 2, [pltpu.VMEM((NR, NC), BF16)], flops=2 * PASS * DIM, trans=PASS
    )(a_unit, b_t)[0]
    msg, base = call(
        col_kernel,
        [VM] * 6,
        [sds(NZY, 40, 128), sds(8, 128)],
        [pltpu.VMEM((16, NR), F32)],
        flops=2 * PASS * 16,
    )(*over_x(pair), la, keep(k_mat))

    parts = lax.all_to_all(msg, "zy", 0, 0)
    msg, base = call(
        row_kernel,
        [VM] * 4,
        [sds(16, 128), sds(8, 128)],
        [pltpu.VMEM((16, NC), F32)],
        flops=2 * PASS * 16,
    )(parts, lb, keep(kt_mat), base)

    pair = call(pair_kernel, [VM] * 2, [sds(16, 128)])(msg, lax.ppermute(msg, "core", swap))[0]
    msg, sums, base = call(
        last_col_kernel,
        [VM] * 8,
        [sds(NZY, 40, 128), sds(NZY, DIM, CH, dtype=BF16), sds(8, 128)],
        [pltpu.VMEM((16, NR), F32), pltpu.VMEM((144, NR), BF16)],
        flops=2 * PASS * 144,
    )(*over_x(pair), la, keep(k_mat), base, a_t)
    parts = lax.all_to_all(msg, "zy", 0, 0)
    own, other, own_pot, total, base, sums = call(
        row_flow_kernel,
        [SM] + [VM] * 5 + [ANY],
        [
            sds(144, 512, dtype=BF16),
            sds(144, 512, dtype=BF16),
            sds(32, 128),
            sds(32, 128),
            sds(8, 128),
            sds(NZY, DIM, CH, dtype=BF16),
        ],
        [pltpu.VMEM((16, NC), F32), pltpu.VMEM((144, NC), BF16), pltpu.VMEM((144, NR), F32)],
        flops=2 * PASS * 144,
        passes={6: 5},
    )(place, parts, lb, keep(kt_mat), base, b_t, sums)

    received = lax.ppermute(other, "core", swap)
    sums = lax.all_to_all(sums, "zy", 0, 0)
    other_pot = lax.ppermute(own_pot, "core", swap)
    mine = call(merge_kernel, [VM] * 2, [sds(144, 512, dtype=BF16)])(own, received)[0]
    others = over_x(mine)[1:]
    flow_a, pot_a = call(
        final_a_kernel, [VM] * 7, [sds(512, DIM), sds(4, 128)]
    )(mine, *others, a_own, la_own, base)
    flow_b, pot_b = call(
        final_b_kernel, [SM] + [VM] * 6, [sds(CH, DIM), sds(64, 128)]
    )(place, sums, parts, total, b_t, own_pot, other_pot)
    return (pot_a.reshape(512), pot_b.reshape(8192), flow_a, flow_b)


def solution(mesh):
    fine = Mesh(mesh.devices.reshape(NZY, 2, 4), ("zy", "core", "x"))
    wide = ("zy", "core")
    return jax.shard_map(
        on_device,
        mesh=fine,
        in_specs=(P(wide, None), P("x", None), P(wide), P("x"), P("x")),
        out_specs=(P(wide), P("x"), P(wide, None), P(("x", "zy", "core"), None)),
        check_vma=False,
    )
```

```python
import functools
import math

import jax
import jax.numpy as jnp
from jax import lax
from jax.experimental import pallas as pl
from jax.experimental.pallas import tpu as pltpu
from jax.sharding import Mesh, PartitionSpec as P

EPS = 0.05
LOG2E = math.log2(math.e)
C2 = LOG2E / EPS
TOP = 50.0
DIM = 128
F32 = jnp.float32
BF16 = jnp.bfloat16


NR = 1024
NC = 4096
CH = 256
NK = NC // CH
NPEER = 8
NZY = 16


def nt(left, right):
    return lax.dot_general(left, right, (((1,), (1,)), ((), ())), preferred_element_type=F32)


def nn(left, right):
    return lax.dot_general(left, right, (((1,), (0,)), ((), ())), preferred_element_type=F32)


def split_rows(vec, rows_ref):
    high = vec.astype(BF16).astype(F32)
    low = vec - high
    for r in range(vec.shape[0]):
        rows_ref[0:1, r * 128 : (r + 1) * 128] = high[r : r + 1, :]
        rows_ref[1:2, r * 128 : (r + 1) * 128] = low[r : r + 1, :]


def combine(parts_ref, count, rows):
    shifts = [parts_ref[d, rows : rows + 8, :] for d in range(count)]
    top = functools.reduce(jnp.maximum, shifts)
    total = None
    for d in range(count):
        half = jnp.exp2(0.5 * (shifts[d][0:1, :] - top[0:1, :]))
        term = parts_ref[d, 0:rows, :] * half * half
        total = term if total is None else total + term
    return total, top


def pair_sum(terms):
    while len(terms) > 1:
        terms = [terms[i] + terms[i + 1] for i in range(0, len(terms), 2)]
    return terms[0]


def pick_cols(ref, core, out_ref):
    for k in range(NK):
        first = ref[4 * k : 4 * k + 2, :]
        second = ref[4 * k + 2 : 4 * k + 4, :]
        out_ref[2 * k : 2 * k + 2, :] = jnp.where(core == 0, first, second)


def unit_t(raw):
    norm = jnp.sqrt(jnp.sum(raw * raw, axis=0, keepdims=True) + 1e-06)
    return (raw / norm).astype(BF16)


def prep_kernel(desc_b, g_all, lb_all, desc_a, la_all, bt_out, at_out, rows_out, shift_out, lb_out, la_out,
                b_raw, a_raw, g_raw, lb_raw, vec, rows, sems):
    core = lax.axis_index("core")
    copies = [
        pltpu.make_async_copy(g_all, g_raw, sems.at[NK]),
        pltpu.make_async_copy(desc_a, a_raw, sems.at[NK + 1]),
        pltpu.make_async_copy(lb_all, lb_raw, sems.at[NK + 2]),
        pltpu.make_async_copy(la_all, la_out, sems.at[NK + 3]),
    ]
    loads = [pltpu.make_async_copy(desc_b.at[k, core], b_raw.at[k], sems.at[k]) for k in range(NK)]
    for copy in copies + loads:
        copy.start()
    rows[...] = jnp.zeros_like(rows)
    for copy in copies:
        copy.wait()
    pick_cols(lb_raw, core, lb_out)
    pick_cols(g_raw, core, vec)
    pot = vec[...] * C2
    shift = jnp.max(jnp.max(pot, axis=0, keepdims=True), axis=1, keepdims=True)
    shift_out[...] = jnp.broadcast_to(shift, (8, 128))
    split_rows(jnp.exp2(pot - shift + TOP), rows)
    rows_out[...] = rows[...].astype(BF16)
    for m in range(2):
        span = slice(m * 256, (m + 1) * 256)
        at_out[:, span] = unit_t(a_raw[span, :].T.astype(F32))
    for k in range(NK):
        loads[k].wait()
        bt_out[:, k * CH : (k + 1) * CH] = unit_t(b_raw[k].T.astype(F32))


def tn(left, right):
    return lax.dot_general(left, right, (((0,), (0,)), ((), ())), preferred_element_type=F32)


def fill_exponentials(left_t, right_t, out):
    for q in range(left_t.shape[1] // 512):
        left = left_t[:, q * 512 : (q + 1) * 512]
        for m in range(right_t.shape[1] // 256):
            span = slice(m * 256, (m + 1) * 256)
            out[q * 512 : (q + 1) * 512, span] = jnp.exp2(tn(left, right_t[:, span]) * (2.0 * C2)).astype(BF16)


def first_kernel(at_own, other_a, la_own, b_t, rows, shift, kt_out, at_out, msg):
    core = lax.axis_index("core")
    for m in range(2):
        span = slice(m * 256, (m + 1) * 256)
        for half, unit in ((core, at_own[:, span]), (1 - core, unit_t(other_a[span, :].T.astype(F32)))):
            at_out[:, pl.ds(pl.multiple_of(half * 512 + m * 256, 256), 256)] = unit
    msg[16:20, :] = la_own[...]
    msg[20:24, :] = la_own[...]
    fill_exponentials(b_t, at_out, kt_out)
    put_rows(msg, nn(rows[...], kt_out[...]), shift[0:1, :])


def put_rows(msg, part, shift):
    part = part[0:1, :] + part[1:2, :]
    for r in range(8):
        msg[r : r + 1, :] = part[:, r * 128 : (r + 1) * 128]
    msg[8:16, :] = jnp.broadcast_to(shift, (8, 128))


def merge_rows(parts):
    shifts = [p[8:16, :] for p in parts]
    top = functools.reduce(jnp.maximum, shifts)
    terms = []
    for part, shift in zip(parts, shifts):
        half = jnp.exp2(0.5 * (shift - top))
        terms.append(part[0:8, :] * half * half)
    return pair_sum(terms), top


def first_pair_kernel(own, received, out, la_out):
    core = lax.axis_index("core")
    pair_kernel(own, received, out)
    mine, theirs = own[16:20, :], received[16:20, :]
    la_out[0:4, :] = jnp.where(core == 0, mine, theirs)
    la_out[4:8, :] = jnp.where(core == 0, theirs, mine)


def pair_kernel(own, received, out):
    total, top = merge_rows([own, received])
    out[0:8, :] = total
    out[8:16, :] = top


def kernel_matrix(a_t, b_t, k_out):
    fill_exponentials(a_t, b_t, k_out)


def row_scales(parts, la, rows):
    total, top = merge_rows(parts)
    level = la[...] * LOG2E - jnp.log2(total)
    shift = jnp.max(jnp.max(level, axis=0, keepdims=True), axis=1, keepdims=True)
    rows[...] = jnp.zeros_like(rows)
    scale = jnp.exp2(level - shift + TOP)
    split_rows(scale, rows)
    return scale, shift, top


def send_all(msg, shift):
    sums = msg[0, 0:32, :]
    for d in range(NZY):
        msg[d, 0:32, :] = sums
        msg[d, 32:40, :] = jnp.broadcast_to(shift, (8, 128))


def send_cols(msg, part, shift):
    part = part[0:1, :] + part[1:2, :]
    for r in range(32):
        msg[0, r : r + 1, :] = part[:, r * 128 : (r + 1) * 128]
    send_all(msg, shift)


def col_kernel(p0, p1, p2, p3, la, k_mat, msg, base_out, rows):
    scale, shift, top = row_scales([p0, p2, p1, p3], la, rows)
    base_out[...] = top
    send_cols(msg, nn(rows[...].astype(BF16), k_mat[...]), shift)


def last_col_kernel(p0, p1, p2, p3, la, k_mat, base, a_t, msg, sums_out, base_out, rows, lhs):
    scale, shift, top = row_scales([p0, p2, p1, p3], la, rows)
    base_out[...] = base[...] + top
    scale = rows[0:1, :] + rows[1:2, :]
    lhs[0:128, :] = (a_t[...].astype(F32) * scale).astype(BF16)
    lhs[128:144, :] = rows[...].astype(BF16)
    for k in range(NK):
        part = nn(lhs[...], k_mat[:, k * CH : (k + 1) * CH])
        sums_out[k] = part[0:128, :].astype(BF16)
        total = part[128:129, :] + part[129:130, :]
        msg[0, 2 * k : 2 * k + 1, :] = total[:, 0:128]
        msg[0, 2 * k + 1 : 2 * k + 2, :] = total[:, 128:256]
    send_all(msg, shift)


def col_scales(parts, lb, rows):
    total, top = combine(parts, NZY, 32)
    log_total = jnp.log2(total)
    level = lb[...] * LOG2E - log_total
    shift = jnp.max(jnp.max(level, axis=0, keepdims=True), axis=1, keepdims=True)
    shift = jnp.ceil(shift)
    rows[...] = jnp.zeros_like(rows)
    split_rows(jnp.exp2(level - shift + TOP), rows)
    return level, total, shift, top


def row_kernel(parts, lb, kt_mat, base, msg, base_out, rows):
    level, total, shift, top = col_scales(parts, lb, rows)
    base_out[...] = base[...] - top
    put_rows(msg, nn(rows[...].astype(BF16), kt_mat[...]), shift)


def pack_rows(out_ref, flow, total, shift):
    n = flow.shape[1]
    out_ref[0:128, :] = flow.astype(BF16)
    high = total.astype(BF16).astype(F32)
    kind = lax.broadcasted_iota(jnp.int32, (16, n), 0)
    tail = jnp.where(kind == 0, high, jnp.where(kind == 1, total - high, jnp.where(kind == 2, shift, 0.0)))
    out_ref[128:144, :] = tail.astype(BF16)


def row_flow_kernel(parts, lb, kt_mat, base, b_t, held, own_out, other_out, pot_out, total_out, base_out, held_out,
                    rows, lhs, acc):
    core = lax.axis_index("core")
    level, total, shift, top = col_scales(parts, lb, rows)
    level_base = base[...] - top
    base_out[...] = level_base
    pot_out[...] = (level + level_base[0:1, :]) * (1.0 / C2)
    total_out[...] = total
    scale = rows[0:1, :] + rows[1:2, :]
    lhs[0:128, :] = (b_t[...].astype(F32) * scale).astype(BF16)
    lhs[128:144, :] = rows[...].astype(BF16)
    acc[...] = nn(lhs[...], kt_mat[...])
    for half, out in ((core, own_out), (1 - core, other_out)):
        part = acc[:, pl.ds(pl.multiple_of(half * 512, 512), 512)]
        pack_rows(out, part[0:128, :], part[128:129, :] + part[129:130, :], shift)


def merge(parts):
    tails = [p[128:144, :].astype(F32) for p in parts]
    shifts = [t[2:3, :] for t in tails]
    top = functools.reduce(jnp.maximum, shifts)
    flows, totals = [], []
    for p, t, s in zip(parts, tails, shifts):
        half = jnp.exp2(0.5 * (s - top))
        flows.append(p[0:128, :].astype(F32) * half * half)
        totals.append((t[0:1, :] + t[1:2, :]) * half * half)
    return pair_sum(flows), pair_sum(totals), top


def merge_kernel(own, received, out):
    flow, total, top = merge([own, received])
    pack_rows(out, flow, total, top)


def final_a_kernel(p0, p1, p2, p3, at_own, la, base, flow_out, pot_out):
    flow, total, top = merge([p0, p2, p1, p3])
    flow_t = flow / total
    level = jnp.log2(total) + (top - TOP - 2.0 * C2)
    for r in range(4):
        here = slice(r * 128, (r + 1) * 128)
        flow_out[here, :] = (flow_t[:, here] - at_own[:, here].astype(F32)).T
        pot_out[r : r + 1, :] = (la[r : r + 1, :] * LOG2E - level[:, here] - base[0:1, :]) * (1.0 / C2)


def final_b_kernel(sums, parts, total, b_t, own_pot, other_pot, flow_out, pot_out):
    core = lax.axis_index("core")
    chunk = lax.axis_index("zy")
    shifts = [parts[d, 32:40, :] for d in range(NZY)]
    top = functools.reduce(jnp.maximum, shifts)
    acc = 0.0
    for d in range(NZY):
        half = jnp.exp2(0.5 * (shifts[d][0:1, 0:1] - top[0:1, 0:1]))
        acc = acc + sums[d].astype(F32) * half * half
    at = pl.multiple_of(chunk * CH, CH)
    unit = b_t[:, pl.ds(at, CH)].astype(F32)
    for r in range(2):
        here = slice(r * 128, (r + 1) * 128)
        denom = total[pl.ds(chunk * 2 + r, 1), :]
        flow_out[here, :] = (acc[:, here] / denom - unit[:, here]).T
    for k in range(NK):
        mine = own_pot[2 * k : 2 * k + 2, :]
        theirs = other_pot[2 * k : 2 * k + 2, :]
        pot_out[4 * k : 4 * k + 2, :] = jnp.where(core == 0, mine, theirs)
        pot_out[4 * k + 2 : 4 * k + 4, :] = jnp.where(core == 0, theirs, mine)


def sds(*shape, dtype=F32):
    return jax.ShapeDtypeStruct(shape, dtype)


VM = pl.BlockSpec(memory_space=pltpu.VMEM)
HB = pl.BlockSpec(memory_space=pltpu.HBM)
ANY = pl.BlockSpec(memory_space=pl.ANY)


def call(kernel, ins, outs, scratch=(), flops=0, bytes_accessed=0, trans=0, passes=None):
    return pl.pallas_call(
        kernel,
        in_specs=ins,
        out_specs=[ANY if i in (passes or {}).values() else VM for i in range(len(outs))],
        input_output_aliases=passes or {},
        out_shape=outs,
        scratch_shapes=list(scratch),
        compiler_params=pltpu.CompilerParams(vmem_limit_bytes=16 * 1024 * 1024),
        cost_estimate=pl.CostEstimate(flops=flops, bytes_accessed=bytes_accessed, transcendentals=trans),
    )


PASS = NR * NC


def on_device(desc_a, desc_b, logmass_a, logmass_b, g_start):
    swap = [(0, 1), (1, 0)]
    ring = [[(i, (i + s) % 4) for i in range(4)] for s in range(4)]
    keep = lambda x: pltpu.with_memory_space_constraint(x, pltpu.VMEM)
    stay = lambda x: pltpu.with_memory_space_constraint(x, pltpu.HBM)
    other_a = lax.ppermute(desc_a, "core", swap)

    b_t, at_own, rows, shift, lb, la_own = call(
        prep_kernel,
        [HB] * 5,
        [
            sds(DIM, NC, dtype=BF16),
            sds(DIM, 512, dtype=BF16),
            sds(16, NC, dtype=BF16),
            sds(8, 128),
            sds(32, 128),
            sds(4, 128),
        ],
        [
            pltpu.VMEM((NK, CH, DIM), BF16),
            pltpu.VMEM((512, DIM), BF16),
            pltpu.VMEM((64, 128), F32),
            pltpu.VMEM((64, 128), F32),
            pltpu.VMEM((32, 128), F32),
            pltpu.VMEM((16, NC), F32),
            pltpu.SemaphoreType.DMA((NK + 4,)),
        ],
        flops=8 * NC * DIM,
        bytes_accessed=2 * NC * DIM,
    )(
        stay(desc_b.reshape(NK, 2, CH, DIM)),
        stay(g_start.reshape(64, 128)),
        stay(logmass_b.reshape(64, 128)),
        stay(desc_a),
        stay(logmass_a.reshape(4, 128)),
    )

    kt_mat, a_t, msg = call(
        first_kernel,
        [VM] * 6,
        [pltpu.VMEM((NC, NR), BF16), sds(DIM, NR, dtype=BF16), sds(24, 128)],
        flops=2 * PASS * DIM,
        trans=PASS,
    )(at_own, other_a, la_own, b_t, rows, shift)

    def over_x(pair):
        return [pair] + [lax.ppermute(pair, "x", ring[s]) for s in (1, 2, 3)]

    pair, la = call(first_pair_kernel, [VM] * 2, [sds(16, 128), sds(8, 128)])(msg, lax.ppermute(msg, "core", swap))
    k_mat = call(
        kernel_matrix, [VM] * 2, [pltpu.VMEM((NR, NC), BF16)], flops=2 * PASS * DIM, trans=PASS
    )(a_t, b_t)[0]
    msg, base = call(
        col_kernel,
        [VM] * 6,
        [sds(NZY, 40, 128), sds(8, 128)],
        [pltpu.VMEM((16, NR), F32)],
        flops=2 * PASS * 16,
    )(*over_x(pair), la, keep(k_mat))

    parts = lax.all_to_all(msg, "zy", 0, 0)
    msg, base = call(
        row_kernel,
        [VM] * 4,
        [sds(16, 128), sds(8, 128)],
        [pltpu.VMEM((16, NC), F32)],
        flops=2 * PASS * 16,
    )(parts, lb, keep(kt_mat), base)

    pair = call(pair_kernel, [VM] * 2, [sds(16, 128)])(msg, lax.ppermute(msg, "core", swap))[0]
    msg, sums, base = call(
        last_col_kernel,
        [VM] * 8,
        [sds(NZY, 40, 128), sds(NZY, DIM, CH, dtype=BF16), sds(8, 128)],
        [pltpu.VMEM((16, NR), F32), pltpu.VMEM((144, NR), BF16)],
        flops=2 * PASS * 144,
    )(*over_x(pair), la, keep(k_mat), base, a_t)
    parts = lax.all_to_all(msg, "zy", 0, 0)
    own, other, own_pot, total, base, sums = call(
        row_flow_kernel,
        [VM] * 5 + [ANY],
        [
            sds(144, 512, dtype=BF16),
            sds(144, 512, dtype=BF16),
            sds(32, 128),
            sds(32, 128),
            sds(8, 128),
            sds(NZY, DIM, CH, dtype=BF16),
        ],
        [pltpu.VMEM((16, NC), F32), pltpu.VMEM((144, NC), BF16), pltpu.VMEM((144, NR), F32)],
        flops=2 * PASS * 144,
        passes={5: 5},
    )(parts, lb, keep(kt_mat), base, b_t, sums)

    received = lax.ppermute(other, "core", swap)
    sums = lax.all_to_all(sums, "zy", 0, 0)
    other_pot = lax.ppermute(own_pot, "core", swap)
    mine = call(merge_kernel, [VM] * 2, [sds(144, 512, dtype=BF16)])(own, received)[0]
    others = over_x(mine)[1:]
    flow_a, pot_a = call(
        final_a_kernel, [VM] * 7, [sds(512, DIM), sds(4, 128)]
    )(mine, *others, at_own, la_own, base)
    flow_b, pot_b = call(
        final_b_kernel, [VM] * 6, [sds(CH, DIM), sds(64, 128)]
    )(sums, parts, total, b_t, own_pot, other_pot)
    return (pot_a.reshape(512), pot_b.reshape(8192), flow_a, flow_b)


def solution(mesh):
    fine = Mesh(mesh.devices.reshape(NZY, 2, 4), ("zy", "core", "x"))
    wide = ("zy", "core")
    return jax.shard_map(
        on_device,
        mesh=fine,
        in_specs=(P(wide, None), P("x", None), P(wide), P("x"), P("x")),
        out_specs=(P(wide), P("x"), P(wide, None), P(("x", "zy", "core"), None)),
        check_vma=False,
    )
```

```python
import functools
import math

import jax
import jax.numpy as jnp
from jax import lax
from jax.experimental import pallas as pl
from jax.experimental.pallas import tpu as pltpu
from jax.sharding import Mesh, PartitionSpec as P

EPS = 0.05
LOG2E = math.log2(math.e)
C2 = LOG2E / EPS
TOP = 50.0
DIM = 128
F32 = jnp.float32
BF16 = jnp.bfloat16


NR = 1024
NC = 4096
CH = 256
NK = NC // CH
NPEER = 8
NZY = 16


def nt(left, right):
    return lax.dot_general(left, right, (((1,), (1,)), ((), ())), preferred_element_type=F32)


def nn(left, right):
    return lax.dot_general(left, right, (((1,), (0,)), ((), ())), preferred_element_type=F32)


def split_rows(vec, rows_ref):
    high = vec.astype(BF16).astype(F32)
    low = vec - high
    for r in range(vec.shape[0]):
        rows_ref[0:1, r * 128 : (r + 1) * 128] = high[r : r + 1, :]
        rows_ref[1:2, r * 128 : (r + 1) * 128] = low[r : r + 1, :]


def combine(parts_ref, count, rows):
    shifts = [parts_ref[d, rows : rows + 8, :] for d in range(count)]
    top = functools.reduce(jnp.maximum, shifts)
    total = None
    for d in range(count):
        half = jnp.exp2(0.5 * (shifts[d][0:1, :] - top[0:1, :]))
        term = parts_ref[d, 0:rows, :] * half * half
        total = term if total is None else total + term
    return total, top


def pair_sum(terms):
    while len(terms) > 1:
        terms = [terms[i] + terms[i + 1] for i in range(0, len(terms), 2)]
    return terms[0]


def pick_cols(ref, core, out_ref):
    for k in range(NK):
        first = ref[4 * k : 4 * k + 2, :]
        second = ref[4 * k + 2 : 4 * k + 4, :]
        out_ref[2 * k : 2 * k + 2, :] = jnp.where(core == 0, first, second)


def unit_t(raw):
    norm = jnp.sqrt(jnp.sum(raw * raw, axis=0, keepdims=True) + 1e-06)
    return (raw / norm).astype(BF16)


def prep_kernel(desc_b, g_all, lb_all, desc_a, la_all, bt_out, at_out, scale_out, shift_out, lb_out, la_out,
                b_raw, a_raw, g_raw, lb_raw, vec, sems):
    core = lax.axis_index("core")
    half = NK // 2
    load_g = pltpu.make_async_copy(g_all, g_raw, sems.at[0])
    load_a = pltpu.make_async_copy(desc_a, a_raw, sems.at[1])
    load_lb = pltpu.make_async_copy(lb_all, lb_raw, sems.at[2])
    load_la = pltpu.make_async_copy(la_all, la_out, sems.at[3])
    loads = [
        pltpu.make_async_copy(desc_b.at[pl.ds(q * half, half), core], b_raw.at[pl.ds(q * half, half)], sems.at[4 + q])
        for q in range(2)
    ]
    for copy in (load_g, loads[0], load_a, loads[1], load_lb, load_la):
        copy.start()
    load_g.wait()
    pick_cols(g_raw, core, vec)
    pot = vec[...] * C2
    shift = jnp.max(jnp.max(pot, axis=0, keepdims=True), axis=1, keepdims=True)
    shift_out[...] = jnp.broadcast_to(shift, (8, 128))
    scale = jnp.exp2(pot - shift + TOP)
    for r in range(32):
        scale_out[r * 128 : (r + 1) * 128, :] = jnp.broadcast_to(scale[r : r + 1, :], (128, 128)).T
    load_a.wait()
    for m in range(2):
        span = slice(m * 256, (m + 1) * 256)
        at_out[:, span] = unit_t(a_raw[span, :].T.astype(F32))
    for q in range(2):
        loads[q].wait()
        for k in range(q * half, (q + 1) * half):
            bt_out[:, k * CH : (k + 1) * CH] = unit_t(b_raw[k].T.astype(F32))
    load_lb.wait()
    load_la.wait()
    pick_cols(lb_raw, core, lb_out)


def tn(left, right):
    return lax.dot_general(left, right, (((0,), (0,)), ((), ())), preferred_element_type=F32)


def fill_exponentials(left_t, right_t, out):
    for q in range(left_t.shape[1] // 512):
        left = left_t[:, q * 512 : (q + 1) * 512]
        for m in range(right_t.shape[1] // 256):
            span = slice(m * 256, (m + 1) * 256)
            out[q * 512 : (q + 1) * 512, span] = jnp.exp2(tn(left, right_t[:, span]) * (2.0 * C2)).astype(BF16)


def first_kernel(at_own, other_a, la_own, b_t, scales, shift, kt_out, at_out, msg):
    core = lax.axis_index("core")
    for m in range(2):
        span = slice(m * 256, (m + 1) * 256)
        for half, unit in ((core, at_own[:, span]), (1 - core, unit_t(other_a[span, :].T.astype(F32)))):
            at_out[:, pl.ds(pl.multiple_of(half * 512 + m * 256, 256), 256)] = unit
    sums = [jnp.zeros((8, 256), F32)] * 4
    for q in range(NC // 512):
        here = slice(q * 512, (q + 1) * 512)
        left = b_t[:, here]
        scale = jnp.concatenate([scales[here, :], scales[here, :]], axis=1)
        for m in range(4):
            span = slice(m * 256, (m + 1) * 256)
            part = jnp.exp2(tn(left, at_out[:, span]) * (2.0 * C2))
            kt_out[here, span] = part.astype(BF16)
            sums[m] = sums[m] + jnp.sum((part * scale).reshape(64, 8, 256), axis=0)
    for m in range(4):
        total = jnp.sum(sums[m], axis=0, keepdims=True)
        msg[2 * m : 2 * m + 1, :] = total[:, 0:128]
        msg[2 * m + 1 : 2 * m + 2, :] = total[:, 128:256]
    msg[8:16, :] = shift[...]
    msg[16:20, :] = la_own[...]
    msg[20:24, :] = la_own[...]


def put_rows(msg, part, shift):
    part = part[0:1, :] + part[1:2, :]
    for r in range(8):
        msg[r : r + 1, :] = part[:, r * 128 : (r + 1) * 128]
    msg[8:16, :] = jnp.broadcast_to(shift, (8, 128))


def merge_rows(parts):
    shifts = [p[8:16, :] for p in parts]
    top = functools.reduce(jnp.maximum, shifts)
    terms = []
    for part, shift in zip(parts, shifts):
        half = jnp.exp2(0.5 * (shift - top))
        terms.append(part[0:8, :] * half * half)
    return pair_sum(terms), top


def first_pair_kernel(own, received, out, la_out):
    core = lax.axis_index("core")
    pair_kernel(own, received, out)
    mine, theirs = own[16:20, :], received[16:20, :]
    la_out[0:4, :] = jnp.where(core == 0, mine, theirs)
    la_out[4:8, :] = jnp.where(core == 0, theirs, mine)


def pair_kernel(own, received, out):
    total, top = merge_rows([own, received])
    out[0:8, :] = total
    out[8:16, :] = top


def kernel_matrix(a_t, b_t, k_out):
    fill_exponentials(a_t, b_t, k_out)


def row_scales(parts, la, rows):
    total, top = merge_rows(parts)
    level = la[...] * LOG2E - jnp.log2(total)
    shift = jnp.max(jnp.max(level, axis=0, keepdims=True), axis=1, keepdims=True)
    rows[...] = jnp.zeros_like(rows)
    scale = jnp.exp2(level - shift + TOP)
    split_rows(scale, rows)
    return scale, shift, top


def send_all(msg, shift):
    sums = msg[0, 0:32, :]
    for d in range(NZY):
        msg[d, 0:32, :] = sums
        msg[d, 32:40, :] = jnp.broadcast_to(shift, (8, 128))


def send_cols(msg, part, shift):
    part = part[0:1, :] + part[1:2, :]
    for r in range(32):
        msg[0, r : r + 1, :] = part[:, r * 128 : (r + 1) * 128]
    send_all(msg, shift)


def col_kernel(p0, p1, p2, p3, la, k_mat, msg, base_out, rows):
    scale, shift, top = row_scales([p0, p2, p1, p3], la, rows)
    base_out[...] = top
    send_cols(msg, nn(rows[...].astype(BF16), k_mat[...]), shift)


def last_col_kernel(p0, p1, p2, p3, la, k_mat, base, a_t, msg, sums_out, base_out, rows, lhs):
    scale, shift, top = row_scales([p0, p2, p1, p3], la, rows)
    base_out[...] = base[...] + top
    scale = rows[0:1, :] + rows[1:2, :]
    lhs[0:128, :] = (a_t[...].astype(F32) * scale).astype(BF16)
    lhs[128:144, :] = rows[...].astype(BF16)
    for k in range(NK):
        part = nn(lhs[...], k_mat[:, k * CH : (k + 1) * CH])
        sums_out[k] = part[0:128, :].astype(BF16)
        total = part[128:129, :] + part[129:130, :]
        msg[0, 2 * k : 2 * k + 1, :] = total[:, 0:128]
        msg[0, 2 * k + 1 : 2 * k + 2, :] = total[:, 128:256]
    send_all(msg, shift)


def col_scales(parts, lb, rows):
    total, top = combine(parts, NZY, 32)
    log_total = jnp.log2(total)
    level = lb[...] * LOG2E - log_total
    shift = jnp.max(jnp.max(level, axis=0, keepdims=True), axis=1, keepdims=True)
    shift = jnp.ceil(shift)
    rows[...] = jnp.zeros_like(rows)
    split_rows(jnp.exp2(level - shift + TOP), rows)
    return level, total, shift, top


def row_kernel(parts, lb, kt_mat, base, msg, base_out, rows):
    level, total, shift, top = col_scales(parts, lb, rows)
    base_out[...] = base[...] - top
    put_rows(msg, nn(rows[...].astype(BF16), kt_mat[...]), shift)


def pack_rows(out_ref, flow, total, shift):
    n = flow.shape[1]
    out_ref[0:128, :] = flow.astype(BF16)
    high = total.astype(BF16).astype(F32)
    kind = lax.broadcasted_iota(jnp.int32, (16, n), 0)
    tail = jnp.where(kind == 0, high, jnp.where(kind == 1, total - high, jnp.where(kind == 2, shift, 0.0)))
    out_ref[128:144, :] = tail.astype(BF16)


def row_flow_kernel(parts, lb, kt_mat, base, b_t, held, own_out, other_out, pot_out, total_out, base_out, held_out,
                    rows, lhs, acc, sem):
    copy = pltpu.make_async_copy(held, held_out, sem)
    copy.start()
    core = lax.axis_index("core")
    level, total, shift, top = col_scales(parts, lb, rows)
    level_base = base[...] - top
    base_out[...] = level_base
    pot_out[...] = (level + level_base[0:1, :]) * (1.0 / C2)
    total_out[...] = total
    scale = rows[0:1, :] + rows[1:2, :]
    lhs[0:128, :] = (b_t[...].astype(F32) * scale).astype(BF16)
    lhs[128:144, :] = rows[...].astype(BF16)
    acc[...] = nn(lhs[...], kt_mat[...])
    for half, out in ((core, own_out), (1 - core, other_out)):
        part = acc[:, pl.ds(pl.multiple_of(half * 512, 512), 512)]
        pack_rows(out, part[0:128, :], part[128:129, :] + part[129:130, :], shift)
    copy.wait()


def merge(parts):
    tails = [p[128:144, :].astype(F32) for p in parts]
    shifts = [t[2:3, :] for t in tails]
    top = functools.reduce(jnp.maximum, shifts)
    flows, totals = [], []
    for p, t, s in zip(parts, tails, shifts):
        half = jnp.exp2(0.5 * (s - top))
        flows.append(p[0:128, :].astype(F32) * half * half)
        totals.append((t[0:1, :] + t[1:2, :]) * half * half)
    return pair_sum(flows), pair_sum(totals), top


def merge_kernel(own, received, out):
    flow, total, top = merge([own, received])
    pack_rows(out, flow, total, top)


def final_a(p0, p1, p2, p3, at_own, la, base, flow_out, pot_out):
    flow, total, top = merge([p0, p2, p1, p3])
    flow_t = flow / total
    level = jnp.log2(total) + (top - TOP - 2.0 * C2)
    for r in range(4):
        here = slice(r * 128, (r + 1) * 128)
        flow_out[here, :] = (flow_t[:, here] - at_own[:, here].astype(F32)).T
        pot_out[r : r + 1, :] = (la[r : r + 1, :] * LOG2E - level[:, here] - base[0:1, :]) * (1.0 / C2)


def final_kernel(p0, p1, p2, p3, at_own, la, base, sums, parts, total, b_t, own_pot, other_pot,
                 flow_a, pot_a, flow_b, pot_b):
    final_a(p0, p1, p2, p3, at_own, la, base, flow_a, pot_a)
    final_b(sums, parts, total, b_t, own_pot, other_pot, flow_b, pot_b)


def final_b(sums, parts, total, b_t, own_pot, other_pot, flow_out, pot_out):
    core = lax.axis_index("core")
    chunk = lax.axis_index("zy")
    shifts = [parts[d, 32:40, :] for d in range(NZY)]
    top = functools.reduce(jnp.maximum, shifts)
    acc = 0.0
    for d in range(NZY):
        half = jnp.exp2(0.5 * (shifts[d][0:1, 0:1] - top[0:1, 0:1]))
        acc = acc + sums[d].astype(F32) * half * half
    at = pl.multiple_of(chunk * CH, CH)
    unit = b_t[:, pl.ds(at, CH)].astype(F32)
    for r in range(2):
        here = slice(r * 128, (r + 1) * 128)
        denom = total[pl.ds(chunk * 2 + r, 1), :]
        flow_out[here, :] = (acc[:, here] / denom - unit[:, here]).T
    for k in range(NK):
        mine = own_pot[2 * k : 2 * k + 2, :]
        theirs = other_pot[2 * k : 2 * k + 2, :]
        pot_out[4 * k : 4 * k + 2, :] = jnp.where(core == 0, mine, theirs)
        pot_out[4 * k + 2 : 4 * k + 4, :] = jnp.where(core == 0, theirs, mine)


def sds(*shape, dtype=F32):
    return jax.ShapeDtypeStruct(shape, dtype)


VM = pl.BlockSpec(memory_space=pltpu.VMEM)
HB = pl.BlockSpec(memory_space=pltpu.HBM)


def call(kernel, ins, outs, scratch=(), flops=0, bytes_accessed=0, trans=0, outside=()):
    return pl.pallas_call(
        kernel,
        in_specs=ins,
        out_specs=[HB if i in outside else VM for i in range(len(outs))],
        out_shape=outs,
        scratch_shapes=list(scratch),
        compiler_params=pltpu.CompilerParams(vmem_limit_bytes=16 * 1024 * 1024),
        cost_estimate=pl.CostEstimate(flops=flops, bytes_accessed=bytes_accessed, transcendentals=trans),
    )


PASS = NR * NC


def on_device(desc_a, desc_b, logmass_a, logmass_b, g_start):
    swap = [(0, 1), (1, 0)]
    ring = [[(i, (i + s) % 4) for i in range(4)] for s in range(4)]
    keep = lambda x: pltpu.with_memory_space_constraint(x, pltpu.VMEM)
    stay = lambda x: pltpu.with_memory_space_constraint(x, pltpu.HBM)
    other_a = lax.ppermute(desc_a, "core", swap)

    b_t, at_own, scales, shift, lb, la_own = call(
        prep_kernel,
        [HB] * 5,
        [
            sds(DIM, NC, dtype=BF16),
            sds(DIM, 512, dtype=BF16),
            sds(NC, 128),
            sds(8, 128),
            sds(32, 128),
            sds(4, 128),
        ],
        [
            pltpu.VMEM((NK, CH, DIM), BF16),
            pltpu.VMEM((512, DIM), BF16),
            pltpu.VMEM((64, 128), F32),
            pltpu.VMEM((64, 128), F32),
            pltpu.VMEM((32, 128), F32),
            pltpu.SemaphoreType.DMA((6,)),
        ],
        flops=8 * NC * DIM,
        bytes_accessed=2 * NC * DIM,
    )(
        stay(desc_b.reshape(NK, 2, CH, DIM)),
        stay(g_start.reshape(64, 128)),
        stay(logmass_b.reshape(64, 128)),
        stay(desc_a),
        stay(logmass_a.reshape(4, 128)),
    )

    kt_mat, a_t, msg = call(
        first_kernel,
        [VM] * 6,
        [pltpu.VMEM((NC, NR), BF16), sds(DIM, NR, dtype=BF16), sds(24, 128)],
        flops=2 * PASS * DIM,
        trans=PASS,
    )(at_own, other_a, la_own, b_t, scales, shift)

    def over_x(pair):
        return [pair] + [lax.ppermute(pair, "x", ring[s]) for s in (1, 2, 3)]

    pair, la = call(first_pair_kernel, [VM] * 2, [sds(16, 128), sds(8, 128)])(msg, lax.ppermute(msg, "core", swap))
    k_mat = call(
        kernel_matrix, [VM] * 2, [pltpu.VMEM((NR, NC), BF16)], flops=2 * PASS * DIM, trans=PASS
    )(a_t, b_t)[0]
    msg, base = call(
        col_kernel,
        [VM] * 6,
        [sds(NZY, 40, 128), sds(8, 128)],
        [pltpu.VMEM((16, NR), F32)],
        flops=2 * PASS * 16,
    )(*over_x(pair), la, keep(k_mat))

    parts = lax.all_to_all(msg, "zy", 0, 0)
    msg, base = call(
        row_kernel,
        [VM] * 4,
        [sds(16, 128), sds(8, 128)],
        [pltpu.VMEM((16, NC), F32)],
        flops=2 * PASS * 16,
    )(parts, lb, keep(kt_mat), base)

    pair = call(pair_kernel, [VM] * 2, [sds(16, 128)])(msg, lax.ppermute(msg, "core", swap))[0]
    msg, sums, base = call(
        last_col_kernel,
        [VM] * 8,
        [sds(NZY, 40, 128), pltpu.VMEM((NZY, DIM, CH), BF16), sds(8, 128)],
        [pltpu.VMEM((16, NR), F32), pltpu.VMEM((144, NR), BF16)],
        flops=2 * PASS * 144,
    )(*over_x(pair), la, keep(k_mat), base, a_t)
    parts = lax.all_to_all(msg, "zy", 0, 0)
    own, other, own_pot, total, base, sums = call(
        row_flow_kernel,
        [VM] * 6,
        [
            sds(144, 512, dtype=BF16),
            sds(144, 512, dtype=BF16),
            sds(32, 128),
            sds(32, 128),
            sds(8, 128),
            pltpu.HBM((NZY, DIM, CH), BF16),
        ],
        [pltpu.VMEM((16, NC), F32), pltpu.VMEM((144, NC), BF16), pltpu.VMEM((144, NR), F32), pltpu.SemaphoreType.DMA],
        flops=2 * PASS * 144,
        outside=(5,),
    )(parts, lb, keep(kt_mat), base, b_t, keep(sums))

    received = lax.ppermute(other, "core", swap)
    sums = lax.all_to_all(sums, "zy", 0, 0)
    other_pot = lax.ppermute(own_pot, "core", swap)
    mine = call(merge_kernel, [VM] * 2, [sds(144, 512, dtype=BF16)])(own, received)[0]
    others = over_x(mine)[1:]
    flow_a, pot_a, flow_b, pot_b = call(
        final_kernel, [VM] * 13, [sds(512, DIM), sds(4, 128), sds(CH, DIM), sds(64, 128)]
    )(mine, *others, at_own, la_own, base, sums, parts, total, b_t, own_pot, other_pot)
    return (pot_a.reshape(512), pot_b.reshape(8192), flow_a, flow_b)


def solution(mesh):
    fine = Mesh(mesh.devices.reshape(NZY, 2, 4), ("zy", "core", "x"))
    wide = ("zy", "core")
    return jax.shard_map(
        on_device,
        mesh=fine,
        in_specs=(P(wide, None), P("x", None), P(wide), P("x"), P("x")),
        out_specs=(P(wide), P("x"), P(wide, None), P(("x", "zy", "core"), None)),
        check_vma=False,
    )
```

```python
import functools
import math

import jax
import jax.numpy as jnp
from jax import lax
from jax.experimental import pallas as pl
from jax.experimental.pallas import tpu as pltpu
from jax.sharding import Mesh, PartitionSpec as P

EPS = 0.05
LOG2E = math.log2(math.e)
C2 = LOG2E / EPS
TOP = 50.0
DIM = 128
F32 = jnp.float32
BF16 = jnp.bfloat16


NR = 1024
NC = 4096
CH = 256
NK = NC // CH
NPEER = 8
NZY = 16


def nt(left, right):
    return lax.dot_general(left, right, (((1,), (1,)), ((), ())), preferred_element_type=F32)


def nn(left, right):
    return lax.dot_general(left, right, (((1,), (0,)), ((), ())), preferred_element_type=F32)


def split_rows(vec, rows_ref):
    high = vec.astype(BF16).astype(F32)
    low = vec - high
    for r in range(vec.shape[0]):
        rows_ref[0:1, r * 128 : (r + 1) * 128] = high[r : r + 1, :]
        rows_ref[1:2, r * 128 : (r + 1) * 128] = low[r : r + 1, :]


def combine(parts_ref, count, rows):
    shifts = [parts_ref[d, rows : rows + 8, :] for d in range(count)]
    top = functools.reduce(jnp.maximum, shifts)
    total = None
    for d in range(count):
        half = jnp.exp2(0.5 * (shifts[d][0:1, :] - top[0:1, :]))
        term = parts_ref[d, 0:rows, :] * half * half
        total = term if total is None else total + term
    return total, top


def pair_sum(terms):
    while len(terms) > 1:
        terms = [terms[i] + terms[i + 1] for i in range(0, len(terms), 2)]
    return terms[0]


def pick_cols(ref, core, out_ref):
    for k in range(NK):
        first = ref[4 * k : 4 * k + 2, :]
        second = ref[4 * k + 2 : 4 * k + 4, :]
        out_ref[2 * k : 2 * k + 2, :] = jnp.where(core == 0, first, second)


def unit_t(raw):
    norm = jnp.sqrt(jnp.sum(raw * raw, axis=0, keepdims=True) + 1e-06)
    return (raw / norm).astype(BF16)


def prep_kernel(desc_b, g_all, lb_all, desc_a, la_all, bt_out, at_out, scale_out, shift_out, lb_out, la_out,
                b_raw, a_raw, g_raw, lb_raw, vec, sems):
    core = lax.axis_index("core")
    half = NK // 2
    load_g = pltpu.make_async_copy(g_all, g_raw, sems.at[0])
    load_a = pltpu.make_async_copy(desc_a, a_raw, sems.at[1])
    load_lb = pltpu.make_async_copy(lb_all, lb_raw, sems.at[2])
    load_la = pltpu.make_async_copy(la_all, la_out, sems.at[3])
    loads = [
        pltpu.make_async_copy(desc_b.at[pl.ds(q * half, half), core], b_raw.at[pl.ds(q * half, half)], sems.at[4 + q])
        for q in range(2)
    ]
    for copy in (load_g, loads[0], load_a, loads[1], load_lb, load_la):
        copy.start()
    load_g.wait()
    pick_cols(g_raw, core, vec)
    pot = vec[...] * C2
    shift = jnp.max(jnp.max(pot, axis=0, keepdims=True), axis=1, keepdims=True)
    shift_out[...] = jnp.broadcast_to(shift, (8, 128))
    scale = jnp.exp2(pot - shift + TOP)
    for r in range(32):
        scale_out[r * 128 : (r + 1) * 128, :] = jnp.broadcast_to(scale[r : r + 1, :], (128, 128)).T
    load_a.wait()
    for m in range(2):
        span = slice(m * 256, (m + 1) * 256)
        at_out[:, span] = unit_t(a_raw[span, :].T.astype(F32))
    for q in range(2):
        loads[q].wait()
        for k in range(q * half, (q + 1) * half):
            bt_out[:, k * CH : (k + 1) * CH] = unit_t(b_raw[k].T.astype(F32))
    load_lb.wait()
    load_la.wait()
    pick_cols(lb_raw, core, lb_out)


def tn(left, right):
    return lax.dot_general(left, right, (((0,), (0,)), ((), ())), preferred_element_type=F32)


def fill_exponentials(left_t, right_t, out):
    for q in range(left_t.shape[1] // 512):
        left = left_t[:, q * 512 : (q + 1) * 512]
        for m in range(right_t.shape[1] // 256):
            span = slice(m * 256, (m + 1) * 256)
            out[q * 512 : (q + 1) * 512, span] = jnp.exp2(tn(left, right_t[:, span]) * (2.0 * C2)).astype(BF16)


def first_kernel(at_own, other_a, la_own, b_t, scales, shift, kt_out, at_out, msg, right):
    core = lax.axis_index("core")
    for m in range(2):
        span = slice(m * 256, (m + 1) * 256)
        for half, unit in ((core, at_own[:, span]), (1 - core, unit_t(other_a[span, :].T.astype(F32)))):
            at_out[:, pl.ds(pl.multiple_of(half * 512 + m * 256, 256), 256)] = unit
    scaled = at_out[...].astype(F32) * (2.0 * C2)
    high = scaled.astype(BF16)
    right[0:DIM, :] = high
    right[DIM : 2 * DIM, :] = (scaled - high.astype(F32)).astype(BF16)
    sums = [jnp.zeros((8, 256), F32)] * 4
    for q in range(NC // 512):
        here = slice(q * 512, (q + 1) * 512)
        left = jnp.concatenate([b_t[:, here].T] * 2, axis=1)
        scale = jnp.concatenate([scales[here, :], scales[here, :]], axis=1)
        for m in range(4):
            span = slice(m * 256, (m + 1) * 256)
            part = jnp.exp2(nn(left, right[:, span]))
            kt_out[here, span] = part.astype(BF16)
            sums[m] = sums[m] + jnp.sum((part * scale).reshape(64, 8, 256), axis=0)
    for m in range(4):
        total = jnp.sum(sums[m], axis=0, keepdims=True)
        msg[2 * m : 2 * m + 1, :] = total[:, 0:128]
        msg[2 * m + 1 : 2 * m + 2, :] = total[:, 128:256]
    msg[8:16, :] = shift[...]
    msg[16:20, :] = la_own[...]
    msg[20:24, :] = la_own[...]


def put_rows(msg, part, shift):
    part = part[0:1, :] + part[1:2, :]
    for r in range(8):
        msg[r : r + 1, :] = part[:, r * 128 : (r + 1) * 128]
    msg[8:16, :] = jnp.broadcast_to(shift, (8, 128))


def merge_rows(parts):
    shifts = [p[8:16, :] for p in parts]
    top = functools.reduce(jnp.maximum, shifts)
    terms = []
    for part, shift in zip(parts, shifts):
        half = jnp.exp2(0.5 * (shift - top))
        terms.append(part[0:8, :] * half * half)
    return pair_sum(terms), top


def first_pair_kernel(own, received, out, la_out):
    core = lax.axis_index("core")
    pair_kernel(own, received, out)
    mine, theirs = own[16:20, :], received[16:20, :]
    la_out[0:4, :] = jnp.where(core == 0, mine, theirs)
    la_out[4:8, :] = jnp.where(core == 0, theirs, mine)


def pair_kernel(own, received, out):
    total, top = merge_rows([own, received])
    out[0:8, :] = total
    out[8:16, :] = top


def kernel_matrix(a_t, b_t, k_out):
    fill_exponentials(a_t, b_t, k_out)


def row_scales(parts, la, rows):
    total, top = merge_rows(parts)
    level = la[...] * LOG2E - jnp.log2(total)
    shift = jnp.max(jnp.max(level, axis=0, keepdims=True), axis=1, keepdims=True)
    rows[...] = jnp.zeros_like(rows)
    scale = jnp.exp2(level - shift + TOP)
    split_rows(scale, rows)
    return scale, shift, top


def send_all(msg, shift):
    sums = msg[0, 0:32, :]
    for d in range(NZY):
        msg[d, 0:32, :] = sums
        msg[d, 32:40, :] = jnp.broadcast_to(shift, (8, 128))


def send_cols(msg, part, shift):
    part = part[0:1, :] + part[1:2, :]
    for r in range(32):
        msg[0, r : r + 1, :] = part[:, r * 128 : (r + 1) * 128]
    send_all(msg, shift)


def col_kernel(p0, p1, p2, p3, la, k_mat, msg, base_out, rows):
    scale, shift, top = row_scales([p0, p2, p1, p3], la, rows)
    base_out[...] = top
    send_cols(msg, nn(rows[...].astype(BF16), k_mat[...]), shift)


def last_col_kernel(p0, p1, p2, p3, la, k_mat, base, a_t, msg, sums_out, base_out, rows, lhs):
    scale, shift, top = row_scales([p0, p2, p1, p3], la, rows)
    base_out[...] = base[...] + top
    scale = rows[0:1, :] + rows[1:2, :]
    lhs[0:128, :] = (a_t[...].astype(F32) * scale).astype(BF16)
    lhs[128:144, :] = rows[...].astype(BF16)
    for k in range(NK):
        part = nn(lhs[...], k_mat[:, k * CH : (k + 1) * CH])
        sums_out[k] = part[0:128, :].astype(BF16)
        total = part[128:129, :] + part[129:130, :]
        msg[0, 2 * k : 2 * k + 1, :] = total[:, 0:128]
        msg[0, 2 * k + 1 : 2 * k + 2, :] = total[:, 128:256]
    send_all(msg, shift)


def col_scales(parts, lb, rows):
    total, top = combine(parts, NZY, 32)
    log_total = jnp.log2(total)
    level = lb[...] * LOG2E - log_total
    shift = jnp.max(jnp.max(level, axis=0, keepdims=True), axis=1, keepdims=True)
    shift = jnp.ceil(shift)
    rows[...] = jnp.zeros_like(rows)
    split_rows(jnp.exp2(level - shift + TOP), rows)
    return level, total, shift, top


def row_kernel(parts, lb, kt_mat, base, msg, base_out, rows):
    level, total, shift, top = col_scales(parts, lb, rows)
    base_out[...] = base[...] - top
    put_rows(msg, nn(rows[...].astype(BF16), kt_mat[...]), shift)


def pack_rows(out_ref, flow, total, shift):
    n = flow.shape[1]
    out_ref[0:128, :] = flow.astype(BF16)
    high = total.astype(BF16).astype(F32)
    kind = lax.broadcasted_iota(jnp.int32, (16, n), 0)
    tail = jnp.where(kind == 0, high, jnp.where(kind == 1, total - high, jnp.where(kind == 2, shift, 0.0)))
    out_ref[128:144, :] = tail.astype(BF16)


def row_flow_kernel(parts, lb, kt_mat, base, b_t, held, own_out, other_out, pot_out, total_out, base_out, held_out,
                    rows, lhs, acc, sem):
    copy = pltpu.make_async_copy(held, held_out, sem)
    copy.start()
    core = lax.axis_index("core")
    level, total, shift, top = col_scales(parts, lb, rows)
    level_base = base[...] - top
    base_out[...] = level_base
    pot_out[...] = (level + level_base[0:1, :]) * (1.0 / C2)
    total_out[...] = total
    scale = rows[0:1, :] + rows[1:2, :]
    lhs[0:128, :] = (b_t[...].astype(F32) * scale).astype(BF16)
    lhs[128:144, :] = rows[...].astype(BF16)
    acc[...] = nn(lhs[...], kt_mat[...])
    for half, out in ((core, own_out), (1 - core, other_out)):
        part = acc[:, pl.ds(pl.multiple_of(half * 512, 512), 512)]
        pack_rows(out, part[0:128, :], part[128:129, :] + part[129:130, :], shift)
    copy.wait()


def merge(parts):
    tails = [p[128:144, :].astype(F32) for p in parts]
    shifts = [t[2:3, :] for t in tails]
    top = functools.reduce(jnp.maximum, shifts)
    flows, totals = [], []
    for p, t, s in zip(parts, tails, shifts):
        half = jnp.exp2(0.5 * (s - top))
        flows.append(p[0:128, :].astype(F32) * half * half)
        totals.append((t[0:1, :] + t[1:2, :]) * half * half)
    return pair_sum(flows), pair_sum(totals), top


def merge_kernel(own, received, out):
    flow, total, top = merge([own, received])
    pack_rows(out, flow, total, top)


def final_a(p0, p1, p2, p3, at_own, la, base, flow_out, pot_out):
    flow, total, top = merge([p0, p2, p1, p3])
    flow_t = flow / total
    level = jnp.log2(total) + (top - TOP - 2.0 * C2)
    for r in range(4):
        here = slice(r * 128, (r + 1) * 128)
        flow_out[here, :] = (flow_t[:, here] - at_own[:, here].astype(F32)).T
        pot_out[r : r + 1, :] = (la[r : r + 1, :] * LOG2E - level[:, here] - base[0:1, :]) * (1.0 / C2)


def final_kernel(p0, p1, p2, p3, at_own, la, base, sums, parts, total, b_t, own_pot, other_pot,
                 flow_a, pot_a, flow_b, pot_b):
    final_a(p0, p1, p2, p3, at_own, la, base, flow_a, pot_a)
    final_b(sums, parts, total, b_t, own_pot, other_pot, flow_b, pot_b)


def final_b(sums, parts, total, b_t, own_pot, other_pot, flow_out, pot_out):
    core = lax.axis_index("core")
    chunk = lax.axis_index("zy")
    shifts = [parts[d, 32:40, :] for d in range(NZY)]
    top = functools.reduce(jnp.maximum, shifts)
    acc = 0.0
    for d in range(NZY):
        half = jnp.exp2(0.5 * (shifts[d][0:1, 0:1] - top[0:1, 0:1]))
        acc = acc + sums[d].astype(F32) * half * half
    at = pl.multiple_of(chunk * CH, CH)
    unit = b_t[:, pl.ds(at, CH)].astype(F32)
    for r in range(2):
        here = slice(r * 128, (r + 1) * 128)
        denom = total[pl.ds(chunk * 2 + r, 1), :]
        flow_out[here, :] = (acc[:, here] / denom - unit[:, here]).T
    for k in range(NK):
        mine = own_pot[2 * k : 2 * k + 2, :]
        theirs = other_pot[2 * k : 2 * k + 2, :]
        pot_out[4 * k : 4 * k + 2, :] = jnp.where(core == 0, mine, theirs)
        pot_out[4 * k + 2 : 4 * k + 4, :] = jnp.where(core == 0, theirs, mine)


def sds(*shape, dtype=F32):
    return jax.ShapeDtypeStruct(shape, dtype)


VM = pl.BlockSpec(memory_space=pltpu.VMEM)
HB = pl.BlockSpec(memory_space=pltpu.HBM)


def call(kernel, ins, outs, scratch=(), flops=0, bytes_accessed=0, trans=0, outside=()):
    return pl.pallas_call(
        kernel,
        in_specs=ins,
        out_specs=[HB if i in outside else VM for i in range(len(outs))],
        out_shape=outs,
        scratch_shapes=list(scratch),
        compiler_params=pltpu.CompilerParams(vmem_limit_bytes=16 * 1024 * 1024),
        cost_estimate=pl.CostEstimate(flops=flops, bytes_accessed=bytes_accessed, transcendentals=trans),
    )


PASS = NR * NC


def on_device(desc_a, desc_b, logmass_a, logmass_b, g_start):
    swap = [(0, 1), (1, 0)]
    ring = [[(i, (i + s) % 4) for i in range(4)] for s in range(4)]
    keep = lambda x: pltpu.with_memory_space_constraint(x, pltpu.VMEM)
    stay = lambda x: pltpu.with_memory_space_constraint(x, pltpu.HBM)
    other_a = lax.ppermute(desc_a, "core", swap)

    b_t, at_own, scales, shift, lb, la_own = call(
        prep_kernel,
        [HB] * 5,
        [
            sds(DIM, NC, dtype=BF16),
            sds(DIM, 512, dtype=BF16),
            sds(NC, 128),
            sds(8, 128),
            sds(32, 128),
            sds(4, 128),
        ],
        [
            pltpu.VMEM((NK, CH, DIM), BF16),
            pltpu.VMEM((512, DIM), BF16),
            pltpu.VMEM((64, 128), F32),
            pltpu.VMEM((64, 128), F32),
            pltpu.VMEM((32, 128), F32),
            pltpu.SemaphoreType.DMA((6,)),
        ],
        flops=8 * NC * DIM,
        bytes_accessed=2 * NC * DIM,
    )(
        stay(desc_b.reshape(NK, 2, CH, DIM)),
        stay(g_start.reshape(64, 128)),
        stay(logmass_b.reshape(64, 128)),
        stay(desc_a),
        stay(logmass_a.reshape(4, 128)),
    )

    kt_mat, a_t, msg = call(
        first_kernel,
        [VM] * 6,
        [pltpu.VMEM((NC, NR), BF16), sds(DIM, NR, dtype=BF16), sds(24, 128)],
        [pltpu.VMEM((2 * DIM, NR), BF16)],
        flops=2 * PASS * DIM,
        trans=PASS,
    )(at_own, other_a, la_own, b_t, scales, shift)

    def over_x(pair):
        return [pair] + [lax.ppermute(pair, "x", ring[s]) for s in (1, 2, 3)]

    pair, la = call(first_pair_kernel, [VM] * 2, [sds(16, 128), sds(8, 128)])(msg, lax.ppermute(msg, "core", swap))
    k_mat = call(
        kernel_matrix, [VM] * 2, [pltpu.VMEM((NR, NC), BF16)], flops=2 * PASS * DIM, trans=PASS
    )(a_t, b_t)[0]
    msg, base = call(
        col_kernel,
        [VM] * 6,
        [sds(NZY, 40, 128), sds(8, 128)],
        [pltpu.VMEM((16, NR), F32)],
        flops=2 * PASS * 16,
    )(*over_x(pair), la, keep(k_mat))

    parts = lax.all_to_all(msg, "zy", 0, 0)
    msg, base = call(
        row_kernel,
        [VM] * 4,
        [sds(16, 128), sds(8, 128)],
        [pltpu.VMEM((16, NC), F32)],
        flops=2 * PASS * 16,
    )(parts, lb, keep(kt_mat), base)

    pair = call(pair_kernel, [VM] * 2, [sds(16, 128)])(msg, lax.ppermute(msg, "core", swap))[0]
    msg, sums, base = call(
        last_col_kernel,
        [VM] * 8,
        [sds(NZY, 40, 128), pltpu.VMEM((NZY, DIM, CH), BF16), sds(8, 128)],
        [pltpu.VMEM((16, NR), F32), pltpu.VMEM((144, NR), BF16)],
        flops=2 * PASS * 144,
    )(*over_x(pair), la, keep(k_mat), base, a_t)
    parts = lax.all_to_all(msg, "zy", 0, 0)
    own, other, own_pot, total, base, sums = call(
        row_flow_kernel,
        [VM] * 6,
        [
            sds(144, 512, dtype=BF16),
            sds(144, 512, dtype=BF16),
            sds(32, 128),
            sds(32, 128),
            sds(8, 128),
            pltpu.HBM((NZY, DIM, CH), BF16),
        ],
        [pltpu.VMEM((16, NC), F32), pltpu.VMEM((144, NC), BF16), pltpu.VMEM((144, NR), F32), pltpu.SemaphoreType.DMA],
        flops=2 * PASS * 144,
        outside=(5,),
    )(parts, lb, keep(kt_mat), base, b_t, keep(sums))

    received = lax.ppermute(other, "core", swap)
    sums = lax.all_to_all(sums, "zy", 0, 0)
    other_pot = lax.ppermute(own_pot, "core", swap)
    mine = call(merge_kernel, [VM] * 2, [sds(144, 512, dtype=BF16)])(own, received)[0]
    others = over_x(mine)[1:]
    flow_a, pot_a, flow_b, pot_b = call(
        final_kernel, [VM] * 13, [sds(512, DIM), sds(4, 128), sds(CH, DIM), sds(64, 128)]
    )(mine, *others, at_own, la_own, base, sums, parts, total, b_t, own_pot, other_pot)
    return (pot_a.reshape(512), pot_b.reshape(8192), flow_a, flow_b)


def solution(mesh):
    fine = Mesh(mesh.devices.reshape(NZY, 2, 4), ("zy", "core", "x"))
    wide = ("zy", "core")
    return jax.shard_map(
        on_device,
        mesh=fine,
        in_specs=(P(wide, None), P("x", None), P(wide), P("x"), P("x")),
        out_specs=(P(wide), P("x"), P(wide, None), P(("x", "zy", "core"), None)),
        check_vma=False,
    )
```

```python
import functools
import math

import jax
import jax.numpy as jnp
from jax import lax
from jax.experimental import pallas as pl
from jax.experimental.pallas import tpu as pltpu
from jax.sharding import Mesh, PartitionSpec as P

EPS = 0.05
LOG2E = math.log2(math.e)
C2 = LOG2E / EPS
TOP = 50.0
DIM = 128
F32 = jnp.float32
BF16 = jnp.bfloat16


NR = 1024
NC = 4096
CH = 256
NK = NC // CH
NPEER = 8
NZY = 16


def nt(left, right):
    return lax.dot_general(left, right, (((1,), (1,)), ((), ())), preferred_element_type=F32)


def nn(left, right):
    return lax.dot_general(left, right, (((1,), (0,)), ((), ())), preferred_element_type=F32)


def split_rows(vec, rows_ref):
    high = vec.astype(BF16).astype(F32)
    low = vec - high
    for r in range(vec.shape[0]):
        rows_ref[0:1, r * 128 : (r + 1) * 128] = high[r : r + 1, :]
        rows_ref[1:2, r * 128 : (r + 1) * 128] = low[r : r + 1, :]


def combine(parts_ref, count, rows):
    shifts = [parts_ref[d, rows : rows + 8, :] for d in range(count)]
    top = functools.reduce(jnp.maximum, shifts)
    total = None
    for d in range(count):
        half = jnp.exp2(0.5 * (shifts[d][0:1, :] - top[0:1, :]))
        term = parts_ref[d, 0:rows, :] * half * half
        total = term if total is None else total + term
    return total, top


def pair_sum(terms):
    while len(terms) > 1:
        terms = [terms[i] + terms[i + 1] for i in range(0, len(terms), 2)]
    return terms[0]


def pick_cols(ref, core, out_ref):
    for k in range(NK):
        first = ref[4 * k : 4 * k + 2, :]
        second = ref[4 * k + 2 : 4 * k + 4, :]
        out_ref[2 * k : 2 * k + 2, :] = jnp.where(core == 0, first, second)


def unit_t(raw):
    norm = jnp.sqrt(jnp.sum(raw * raw, axis=0, keepdims=True) + 1e-06)
    return (raw / norm).astype(BF16)


def two_parts(unit):
    scaled = unit.astype(F32) * (2.0 * C2)
    high = scaled.astype(BF16)
    return jnp.concatenate([high, (scaled - high.astype(F32)).astype(BF16)], axis=0)


def prep_kernel(desc_b, g_all, lb_all, desc_a, la_all, bt_out, at_out, right_out, scale_out, shift_out, lb_out, la_out,
                b_raw, a_raw, g_raw, lb_raw, vec, sems):
    core = lax.axis_index("core")
    half = NK // 2
    load_g = pltpu.make_async_copy(g_all, g_raw, sems.at[0])
    load_a = pltpu.make_async_copy(desc_a, a_raw, sems.at[1])
    load_lb = pltpu.make_async_copy(lb_all, lb_raw, sems.at[2])
    load_la = pltpu.make_async_copy(la_all, la_out, sems.at[3])
    loads = [
        pltpu.make_async_copy(desc_b.at[pl.ds(q * half, half), core], b_raw.at[pl.ds(q * half, half)], sems.at[4 + q])
        for q in range(2)
    ]
    for copy in (load_g, loads[0], load_a, loads[1], load_lb, load_la):
        copy.start()
    load_g.wait()
    pick_cols(g_raw, core, vec)
    pot = vec[...] * C2
    shift = jnp.max(jnp.max(pot, axis=0, keepdims=True), axis=1, keepdims=True)
    shift_out[...] = jnp.broadcast_to(shift, (8, 128))
    scale = jnp.exp2(pot - shift + TOP)
    for r in range(32):
        scale_out[r * 128 : (r + 1) * 128, :] = jnp.broadcast_to(scale[r : r + 1, :], (128, 128)).T
    load_a.wait()
    for m in range(2):
        span = slice(m * 256, (m + 1) * 256)
        unit = unit_t(a_raw[span, :].T.astype(F32))
        at_out[:, span] = unit
        right_out[:, span] = two_parts(unit)
    for q in range(2):
        loads[q].wait()
        for k in range(q * half, (q + 1) * half):
            bt_out[:, k * CH : (k + 1) * CH] = unit_t(b_raw[k].T.astype(F32))
    load_lb.wait()
    load_la.wait()
    pick_cols(lb_raw, core, lb_out)


def tn(left, right):
    return lax.dot_general(left, right, (((0,), (0,)), ((), ())), preferred_element_type=F32)


def fill_exponentials(left_t, right_t, out):
    for q in range(left_t.shape[1] // 512):
        left = left_t[:, q * 512 : (q + 1) * 512]
        for m in range(right_t.shape[1] // 256):
            span = slice(m * 256, (m + 1) * 256)
            out[q * 512 : (q + 1) * 512, span] = jnp.exp2(tn(left, right_t[:, span]) * (2.0 * C2)).astype(BF16)


def first_kernel(at_own, right_own, other_a, la_own, b_t, scales, shift, kt_out, at_out, msg, right):
    core = lax.axis_index("core")
    for m in range(2):
        span = slice(m * 256, (m + 1) * 256)
        unit = unit_t(other_a[span, :].T.astype(F32))
        own = pl.ds(pl.multiple_of(core * 512 + m * 256, 256), 256)
        other = pl.ds(pl.multiple_of((1 - core) * 512 + m * 256, 256), 256)
        at_out[:, own] = at_own[:, span]
        at_out[:, other] = unit
        right[:, own] = right_own[:, span]
        right[:, other] = two_parts(unit)
    sums = [jnp.zeros((8, 256), F32)] * 4
    for q in range(NC // 512):
        here = slice(q * 512, (q + 1) * 512)
        left = jnp.concatenate([b_t[:, here].T] * 2, axis=1)
        scale = jnp.concatenate([scales[here, :], scales[here, :]], axis=1)
        for m in range(4):
            span = slice(m * 256, (m + 1) * 256)
            part = jnp.exp2(nn(left, right[:, span]))
            kt_out[here, span] = part.astype(BF16)
            sums[m] = sums[m] + jnp.sum((part * scale).reshape(64, 8, 256), axis=0)
    for m in range(4):
        total = jnp.sum(sums[m], axis=0, keepdims=True)
        msg[2 * m : 2 * m + 1, :] = total[:, 0:128]
        msg[2 * m + 1 : 2 * m + 2, :] = total[:, 128:256]
    msg[8:16, :] = shift[...]
    msg[16:20, :] = la_own[...]
    msg[20:24, :] = la_own[...]


def put_rows(msg, part, shift):
    part = part[0:1, :] + part[1:2, :]
    for r in range(8):
        msg[r : r + 1, :] = part[:, r * 128 : (r + 1) * 128]
    msg[8:16, :] = jnp.broadcast_to(shift, (8, 128))


def merge_rows(parts):
    shifts = [p[8:16, :] for p in parts]
    top = functools.reduce(jnp.maximum, shifts)
    terms = []
    for part, shift in zip(parts, shifts):
        half = jnp.exp2(0.5 * (shift - top))
        terms.append(part[0:8, :] * half * half)
    return pair_sum(terms), top


def first_pair_kernel(own, received, out, la_out):
    core = lax.axis_index("core")
    pair_kernel(own, received, out)
    mine, theirs = own[16:20, :], received[16:20, :]
    la_out[0:4, :] = jnp.where(core == 0, mine, theirs)
    la_out[4:8, :] = jnp.where(core == 0, theirs, mine)


def pair_kernel(own, received, out):
    total, top = merge_rows([own, received])
    out[0:8, :] = total
    out[8:16, :] = top


def kernel_matrix(a_t, b_t, k_out):
    fill_exponentials(a_t, b_t, k_out)


def row_scales(parts, la, rows):
    total, top = merge_rows(parts)
    level = la[...] * LOG2E - jnp.log2(total)
    shift = jnp.max(jnp.max(level, axis=0, keepdims=True), axis=1, keepdims=True)
    rows[...] = jnp.zeros_like(rows)
    scale = jnp.exp2(level - shift + TOP)
    split_rows(scale, rows)
    return scale, shift, top


def send_all(msg, shift):
    sums = msg[0, 0:32, :]
    for d in range(NZY):
        msg[d, 0:32, :] = sums
        msg[d, 32:40, :] = jnp.broadcast_to(shift, (8, 128))


def send_cols(msg, part, shift):
    part = part[0:1, :] + part[1:2, :]
    for r in range(32):
        msg[0, r : r + 1, :] = part[:, r * 128 : (r + 1) * 128]
    send_all(msg, shift)


def col_kernel(p0, p1, p2, p3, la, k_mat, msg, base_out, rows):
    scale, shift, top = row_scales([p0, p2, p1, p3], la, rows)
    base_out[...] = top
    send_cols(msg, nn(rows[...].astype(BF16), k_mat[...]), shift)


def last_col_kernel(p0, p1, p2, p3, la, k_mat, base, a_t, msg, sums_out, base_out, rows, lhs):
    scale, shift, top = row_scales([p0, p2, p1, p3], la, rows)
    base_out[...] = base[...] + top
    scale = rows[0:1, :] + rows[1:2, :]
    lhs[0:128, :] = (a_t[...].astype(F32) * scale).astype(BF16)
    lhs[128:144, :] = rows[...].astype(BF16)
    for k in range(NK):
        part = nn(lhs[...], k_mat[:, k * CH : (k + 1) * CH])
        sums_out[k] = part[0:128, :].astype(BF16)
        total = part[128:129, :] + part[129:130, :]
        msg[0, 2 * k : 2 * k + 1, :] = total[:, 0:128]
        msg[0, 2 * k + 1 : 2 * k + 2, :] = total[:, 128:256]
    send_all(msg, shift)


def col_scales(parts, lb, rows):
    total, top = combine(parts, NZY, 32)
    log_total = jnp.log2(total)
    level = lb[...] * LOG2E - log_total
    shift = jnp.max(jnp.max(level, axis=0, keepdims=True), axis=1, keepdims=True)
    shift = jnp.ceil(shift)
    rows[...] = jnp.zeros_like(rows)
    split_rows(jnp.exp2(level - shift + TOP), rows)
    return level, total, shift, top


def row_kernel(parts, lb, kt_mat, base, msg, base_out, rows):
    level, total, shift, top = col_scales(parts, lb, rows)
    base_out[...] = base[...] - top
    put_rows(msg, nn(rows[...].astype(BF16), kt_mat[...]), shift)


def pack_rows(out_ref, flow, total, shift):
    n = flow.shape[1]
    out_ref[0:128, :] = flow.astype(BF16)
    high = total.astype(BF16).astype(F32)
    kind = lax.broadcasted_iota(jnp.int32, (16, n), 0)
    tail = jnp.where(kind == 0, high, jnp.where(kind == 1, total - high, jnp.where(kind == 2, shift, 0.0)))
    out_ref[128:144, :] = tail.astype(BF16)


def row_flow_kernel(parts, lb, kt_mat, base, b_t, held, own_out, other_out, pot_out, total_out, base_out, held_out,
                    rows, lhs, acc, sem):
    copy = pltpu.make_async_copy(held, held_out, sem)
    copy.start()
    core = lax.axis_index("core")
    level, total, shift, top = col_scales(parts, lb, rows)
    level_base = base[...] - top
    base_out[...] = level_base
    pot_out[...] = (level + level_base[0:1, :]) * (1.0 / C2)
    total_out[...] = total
    scale = rows[0:1, :] + rows[1:2, :]
    lhs[0:128, :] = (b_t[...].astype(F32) * scale).astype(BF16)
    lhs[128:144, :] = rows[...].astype(BF16)
    acc[...] = nn(lhs[...], kt_mat[...])
    for half, out in ((core, own_out), (1 - core, other_out)):
        part = acc[:, pl.ds(pl.multiple_of(half * 512, 512), 512)]
        pack_rows(out, part[0:128, :], part[128:129, :] + part[129:130, :], shift)
    copy.wait()


def merge(parts):
    tails = [p[128:144, :].astype(F32) for p in parts]
    shifts = [t[2:3, :] for t in tails]
    top = functools.reduce(jnp.maximum, shifts)
    flows, totals = [], []
    for p, t, s in zip(parts, tails, shifts):
        half = jnp.exp2(0.5 * (s - top))
        flows.append(p[0:128, :].astype(F32) * half * half)
        totals.append((t[0:1, :] + t[1:2, :]) * half * half)
    return pair_sum(flows), pair_sum(totals), top


def merge_kernel(own, received, out):
    flow, total, top = merge([own, received])
    pack_rows(out, flow, total, top)


def final_a(p0, p1, p2, p3, at_own, la, base, flow_out, pot_out):
    flow, total, top = merge([p0, p2, p1, p3])
    flow_t = flow / total
    level = jnp.log2(total) + (top - TOP - 2.0 * C2)
    for r in range(4):
        here = slice(r * 128, (r + 1) * 128)
        flow_out[here, :] = (flow_t[:, here] - at_own[:, here].astype(F32)).T
        pot_out[r : r + 1, :] = (la[r : r + 1, :] * LOG2E - level[:, here] - base[0:1, :]) * (1.0 / C2)


def final_kernel(p0, p1, p2, p3, at_own, la, base, sums, parts, total, b_t, own_pot, other_pot,
                 flow_a, pot_a, flow_b, pot_b):
    final_a(p0, p1, p2, p3, at_own, la, base, flow_a, pot_a)
    final_b(sums, parts, total, b_t, own_pot, other_pot, flow_b, pot_b)


def final_b(sums, parts, total, b_t, own_pot, other_pot, flow_out, pot_out):
    core = lax.axis_index("core")
    chunk = lax.axis_index("zy")
    shifts = [parts[d, 32:40, :] for d in range(NZY)]
    top = functools.reduce(jnp.maximum, shifts)
    acc = 0.0
    for d in range(NZY):
        half = jnp.exp2(0.5 * (shifts[d][0:1, 0:1] - top[0:1, 0:1]))
        acc = acc + sums[d].astype(F32) * half * half
    at = pl.multiple_of(chunk * CH, CH)
    unit = b_t[:, pl.ds(at, CH)].astype(F32)
    for r in range(2):
        here = slice(r * 128, (r + 1) * 128)
        denom = total[pl.ds(chunk * 2 + r, 1), :]
        flow_out[here, :] = (acc[:, here] / denom - unit[:, here]).T
    for k in range(NK):
        mine = own_pot[2 * k : 2 * k + 2, :]
        theirs = other_pot[2 * k : 2 * k + 2, :]
        pot_out[4 * k : 4 * k + 2, :] = jnp.where(core == 0, mine, theirs)
        pot_out[4 * k + 2 : 4 * k + 4, :] = jnp.where(core == 0, theirs, mine)


def sds(*shape, dtype=F32):
    return jax.ShapeDtypeStruct(shape, dtype)


VM = pl.BlockSpec(memory_space=pltpu.VMEM)
HB = pl.BlockSpec(memory_space=pltpu.HBM)


def call(kernel, ins, outs, scratch=(), flops=0, bytes_accessed=0, trans=0, outside=()):
    return pl.pallas_call(
        kernel,
        in_specs=ins,
        out_specs=[HB if i in outside else VM for i in range(len(outs))],
        out_shape=outs,
        scratch_shapes=list(scratch),
        compiler_params=pltpu.CompilerParams(vmem_limit_bytes=16 * 1024 * 1024),
        cost_estimate=pl.CostEstimate(flops=flops, bytes_accessed=bytes_accessed, transcendentals=trans),
    )


PASS = NR * NC


def on_device(desc_a, desc_b, logmass_a, logmass_b, g_start):
    swap = [(0, 1), (1, 0)]
    ring = [[(i, (i + s) % 4) for i in range(4)] for s in range(4)]
    keep = lambda x: pltpu.with_memory_space_constraint(x, pltpu.VMEM)
    stay = lambda x: pltpu.with_memory_space_constraint(x, pltpu.HBM)
    other_a = lax.ppermute(desc_a, "core", swap)

    b_t, at_own, right_own, scales, shift, lb, la_own = call(
        prep_kernel,
        [HB] * 5,
        [
            sds(DIM, NC, dtype=BF16),
            sds(DIM, 512, dtype=BF16),
            sds(2 * DIM, 512, dtype=BF16),
            sds(NC, 128),
            sds(8, 128),
            sds(32, 128),
            sds(4, 128),
        ],
        [
            pltpu.VMEM((NK, CH, DIM), BF16),
            pltpu.VMEM((512, DIM), BF16),
            pltpu.VMEM((64, 128), F32),
            pltpu.VMEM((64, 128), F32),
            pltpu.VMEM((32, 128), F32),
            pltpu.SemaphoreType.DMA((6,)),
        ],
        flops=8 * NC * DIM,
        bytes_accessed=2 * NC * DIM,
    )(
        stay(desc_b.reshape(NK, 2, CH, DIM)),
        stay(g_start.reshape(64, 128)),
        stay(logmass_b.reshape(64, 128)),
        stay(desc_a),
        stay(logmass_a.reshape(4, 128)),
    )

    kt_mat, a_t, msg = call(
        first_kernel,
        [VM] * 7,
        [pltpu.VMEM((NC, NR), BF16), sds(DIM, NR, dtype=BF16), sds(24, 128)],
        [pltpu.VMEM((2 * DIM, NR), BF16)],
        flops=2 * PASS * DIM,
        trans=PASS,
    )(at_own, right_own, other_a, la_own, b_t, scales, shift)

    def over_x(pair):
        return [pair] + [lax.ppermute(pair, "x", ring[s]) for s in (1, 2, 3)]

    pair, la = call(first_pair_kernel, [VM] * 2, [sds(16, 128), sds(8, 128)])(msg, lax.ppermute(msg, "core", swap))
    k_mat = call(
        kernel_matrix, [VM] * 2, [pltpu.VMEM((NR, NC), BF16)], flops=2 * PASS * DIM, trans=PASS
    )(a_t, b_t)[0]
    msg, base = call(
        col_kernel,
        [VM] * 6,
        [sds(NZY, 40, 128), sds(8, 128)],
        [pltpu.VMEM((16, NR), F32)],
        flops=2 * PASS * 16,
    )(*over_x(pair), la, keep(k_mat))

    parts = lax.all_to_all(msg, "zy", 0, 0)
    msg, base = call(
        row_kernel,
        [VM] * 4,
        [sds(16, 128), sds(8, 128)],
        [pltpu.VMEM((16, NC), F32)],
        flops=2 * PASS * 16,
    )(parts, lb, keep(kt_mat), base)

    pair = call(pair_kernel, [VM] * 2, [sds(16, 128)])(msg, lax.ppermute(msg, "core", swap))[0]
    msg, sums, base = call(
        last_col_kernel,
        [VM] * 8,
        [sds(NZY, 40, 128), pltpu.VMEM((NZY, DIM, CH), BF16), sds(8, 128)],
        [pltpu.VMEM((16, NR), F32), pltpu.VMEM((144, NR), BF16)],
        flops=2 * PASS * 144,
    )(*over_x(pair), la, keep(k_mat), base, a_t)
    parts = lax.all_to_all(msg, "zy", 0, 0)
    own, other, own_pot, total, base, sums = call(
        row_flow_kernel,
        [VM] * 6,
        [
            sds(144, 512, dtype=BF16),
            sds(144, 512, dtype=BF16),
            sds(32, 128),
            sds(32, 128),
            sds(8, 128),
            pltpu.HBM((NZY, DIM, CH), BF16),
        ],
        [pltpu.VMEM((16, NC), F32), pltpu.VMEM((144, NC), BF16), pltpu.VMEM((144, NR), F32), pltpu.SemaphoreType.DMA],
        flops=2 * PASS * 144,
        outside=(5,),
    )(parts, lb, keep(kt_mat), base, b_t, keep(sums))

    received = lax.ppermute(other, "core", swap)
    sums = lax.all_to_all(sums, "zy", 0, 0)
    other_pot = lax.ppermute(own_pot, "core", swap)
    mine = call(merge_kernel, [VM] * 2, [sds(144, 512, dtype=BF16)])(own, received)[0]
    others = over_x(mine)[1:]
    flow_a, pot_a, flow_b, pot_b = call(
        final_kernel, [VM] * 13, [sds(512, DIM), sds(4, 128), sds(CH, DIM), sds(64, 128)]
    )(mine, *others, at_own, la_own, base, sums, parts, total, b_t, own_pot, other_pot)
    return (pot_a.reshape(512), pot_b.reshape(8192), flow_a, flow_b)


def solution(mesh):
    fine = Mesh(mesh.devices.reshape(NZY, 2, 4), ("zy", "core", "x"))
    wide = ("zy", "core")
    return jax.shard_map(
        on_device,
        mesh=fine,
        in_specs=(P(wide, None), P("x", None), P(wide), P("x"), P("x")),
        out_specs=(P(wide), P("x"), P(wide, None), P(("x", "zy", "core"), None)),
        check_vma=False,
    )
```

```python
import functools
import math

import jax
import jax.numpy as jnp
from jax import lax
from jax.experimental import pallas as pl
from jax.experimental.pallas import tpu as pltpu
from jax.sharding import Mesh, PartitionSpec as P

EPS = 0.05
LOG2E = math.log2(math.e)
C2 = LOG2E / EPS
TOP = 50.0
DIM = 128
F32 = jnp.float32
BF16 = jnp.bfloat16


NR = 1024
NC = 4096
CH = 256
NK = NC // CH
NPEER = 8
NZY = 16


def nt(left, right):
    return lax.dot_general(left, right, (((1,), (1,)), ((), ())), preferred_element_type=F32)


def nn(left, right):
    return lax.dot_general(left, right, (((1,), (0,)), ((), ())), preferred_element_type=F32)


def split_rows(vec, rows_ref):
    high = vec.astype(BF16).astype(F32)
    low = vec - high
    for r in range(vec.shape[0]):
        rows_ref[0:1, r * 128 : (r + 1) * 128] = high[r : r + 1, :]
        rows_ref[1:2, r * 128 : (r + 1) * 128] = low[r : r + 1, :]


def combine(parts_ref, count, rows):
    shifts = [parts_ref[d, rows : rows + 8, :] for d in range(count)]
    top = functools.reduce(jnp.maximum, shifts)
    total = None
    for d in range(count):
        half = jnp.exp2(0.5 * (shifts[d][0:1, :] - top[0:1, :]))
        term = parts_ref[d, 0:rows, :] * half * half
        total = term if total is None else total + term
    return total, top


def pair_sum(terms):
    while len(terms) > 1:
        terms = [terms[i] + terms[i + 1] for i in range(0, len(terms), 2)]
    return terms[0]


def pick_cols(ref, core, out_ref):
    for k in range(NK):
        first = ref[4 * k : 4 * k + 2, :]
        second = ref[4 * k + 2 : 4 * k + 4, :]
        out_ref[2 * k : 2 * k + 2, :] = jnp.where(core == 0, first, second)


def unit_t(raw):
    norm = jnp.sqrt(jnp.sum(raw * raw, axis=0, keepdims=True) + 1e-06)
    return (raw / norm).astype(BF16)


def two_parts(unit):
    scaled = unit.astype(F32) * (2.0 * C2)
    high = scaled.astype(BF16)
    return jnp.concatenate([high, (scaled - high.astype(F32)).astype(BF16)], axis=0)


def prep_kernel(desc_b, g_all, lb_all, desc_a, la_all, bt_out, at_out, right_out, scale_out, shift_out, lb_out, la_out,
                b_raw, a_raw, g_raw, lb_raw, vec, sems):
    core = lax.axis_index("core")
    load_g = pltpu.make_async_copy(g_all, g_raw, sems.at[0])
    load_a = pltpu.make_async_copy(desc_a, a_raw, sems.at[1])
    load_lb = pltpu.make_async_copy(lb_all, lb_raw, sems.at[2])
    load_la = pltpu.make_async_copy(la_all, la_out, sems.at[3])
    load_b = pltpu.make_async_copy(desc_b.at[:, core], b_raw, sems.at[4])
    for copy in (load_g, load_a, load_b, load_lb, load_la):
        copy.start()
    load_g.wait()
    pick_cols(g_raw, core, vec)
    pot = vec[...] * C2
    shift = jnp.max(jnp.max(pot, axis=0, keepdims=True), axis=1, keepdims=True)
    shift_out[...] = jnp.broadcast_to(shift, (8, 128))
    scale = jnp.exp2(pot - shift + TOP)
    for r in range(32):
        scale_out[r * 128 : (r + 1) * 128, :] = jnp.broadcast_to(scale[r : r + 1, :], (128, 128)).T
    load_a.wait()
    for m in range(2):
        span = slice(m * 256, (m + 1) * 256)
        unit = unit_t(a_raw[span, :].T.astype(F32))
        at_out[:, span] = unit
        right_out[:, span] = two_parts(unit)
    load_b.wait()
    for k in range(NK):
        bt_out[:, k * CH : (k + 1) * CH] = unit_t(b_raw[k].T.astype(F32))
    load_lb.wait()
    load_la.wait()
    pick_cols(lb_raw, core, lb_out)


def tn(left, right):
    return lax.dot_general(left, right, (((0,), (0,)), ((), ())), preferred_element_type=F32)


def fill_exponentials(left_t, right_t, out):
    for q in range(left_t.shape[1] // 512):
        left = left_t[:, q * 512 : (q + 1) * 512]
        for m in range(right_t.shape[1] // 256):
            span = slice(m * 256, (m + 1) * 256)
            out[q * 512 : (q + 1) * 512, span] = jnp.exp2(tn(left, right_t[:, span]) * (2.0 * C2)).astype(BF16)


def first_kernel(at_own, right_own, other_a, la_own, b_t, scales, shift, kt_out, at_out, msg, right):
    core = lax.axis_index("core")
    for m in range(2):
        span = slice(m * 256, (m + 1) * 256)
        unit = unit_t(other_a[span, :].T.astype(F32))
        own = pl.ds(pl.multiple_of(core * 512 + m * 256, 256), 256)
        other = pl.ds(pl.multiple_of((1 - core) * 512 + m * 256, 256), 256)
        at_out[:, own] = at_own[:, span]
        at_out[:, other] = unit
        right[:, own] = right_own[:, span]
        right[:, other] = two_parts(unit)
    sums = [jnp.zeros((8, 256), F32)] * 4
    for q in range(NC // 512):
        here = slice(q * 512, (q + 1) * 512)
        left = jnp.concatenate([b_t[:, here].T] * 2, axis=1)
        scale = jnp.concatenate([scales[here, :], scales[here, :]], axis=1)
        for m in range(4):
            span = slice(m * 256, (m + 1) * 256)
            part = jnp.exp2(nn(left, right[:, span]))
            kt_out[here, span] = part.astype(BF16)
            sums[m] = sums[m] + jnp.sum((part * scale).reshape(64, 8, 256), axis=0)
    for m in range(4):
        total = jnp.sum(sums[m], axis=0, keepdims=True)
        msg[2 * m : 2 * m + 1, :] = total[:, 0:128]
        msg[2 * m + 1 : 2 * m + 2, :] = total[:, 128:256]
    msg[8:16, :] = shift[...]
    msg[16:20, :] = la_own[...]
    msg[20:24, :] = la_own[...]


def put_rows(msg, part, shift):
    part = part[0:1, :] + part[1:2, :]
    for r in range(8):
        msg[r : r + 1, :] = part[:, r * 128 : (r + 1) * 128]
    msg[8:16, :] = jnp.broadcast_to(shift, (8, 128))


def merge_rows(parts):
    shifts = [p[8:16, :] for p in parts]
    top = functools.reduce(jnp.maximum, shifts)
    terms = []
    for part, shift in zip(parts, shifts):
        half = jnp.exp2(0.5 * (shift - top))
        terms.append(part[0:8, :] * half * half)
    return pair_sum(terms), top


def first_pair_kernel(own, received, out, la_out):
    core = lax.axis_index("core")
    pair_kernel(own, received, out)
    mine, theirs = own[16:20, :], received[16:20, :]
    la_out[0:4, :] = jnp.where(core == 0, mine, theirs)
    la_out[4:8, :] = jnp.where(core == 0, theirs, mine)


def pair_kernel(own, received, out):
    total, top = merge_rows([own, received])
    out[0:8, :] = total
    out[8:16, :] = top


def kernel_matrix(a_t, b_t, k_out):
    fill_exponentials(a_t, b_t, k_out)


def row_scales(parts, la, rows):
    total, top = merge_rows(parts)
    level = la[...] * LOG2E - jnp.log2(total)
    shift = jnp.max(jnp.max(level, axis=0, keepdims=True), axis=1, keepdims=True)
    rows[...] = jnp.zeros_like(rows)
    scale = jnp.exp2(level - shift + TOP)
    split_rows(scale, rows)
    return scale, shift, top


def send_all(msg, shift):
    sums = msg[0, 0:32, :]
    for d in range(NZY):
        msg[d, 0:32, :] = sums
        msg[d, 32:40, :] = jnp.broadcast_to(shift, (8, 128))


def send_cols(msg, part, shift):
    part = part[0:1, :] + part[1:2, :]
    for r in range(32):
        msg[0, r : r + 1, :] = part[:, r * 128 : (r + 1) * 128]
    send_all(msg, shift)


def col_kernel(p0, p1, p2, p3, la, k_mat, msg, base_out, rows):
    scale, shift, top = row_scales([p0, p2, p1, p3], la, rows)
    base_out[...] = top
    send_cols(msg, nn(rows[...].astype(BF16), k_mat[...]), shift)


def last_col_kernel(p0, p1, p2, p3, la, k_mat, base, a_t, msg, sums_out, base_out, rows, lhs):
    scale, shift, top = row_scales([p0, p2, p1, p3], la, rows)
    base_out[...] = base[...] + top
    scale = rows[0:1, :] + rows[1:2, :]
    lhs[0:128, :] = (a_t[...].astype(F32) * scale).astype(BF16)
    lhs[128:144, :] = rows[...].astype(BF16)
    for k in range(NK):
        part = nn(lhs[...], k_mat[:, k * CH : (k + 1) * CH])
        sums_out[k] = part[0:128, :].astype(BF16)
        total = part[128:129, :] + part[129:130, :]
        msg[0, 2 * k : 2 * k + 1, :] = total[:, 0:128]
        msg[0, 2 * k + 1 : 2 * k + 2, :] = total[:, 128:256]
    send_all(msg, shift)


def col_scales(parts, lb, rows):
    total, top = combine(parts, NZY, 32)
    log_total = jnp.log2(total)
    level = lb[...] * LOG2E - log_total
    shift = jnp.max(jnp.max(level, axis=0, keepdims=True), axis=1, keepdims=True)
    shift = jnp.ceil(shift)
    rows[...] = jnp.zeros_like(rows)
    split_rows(jnp.exp2(level - shift + TOP), rows)
    return level, total, shift, top


def row_kernel(parts, lb, kt_mat, base, msg, base_out, rows):
    level, total, shift, top = col_scales(parts, lb, rows)
    base_out[...] = base[...] - top
    put_rows(msg, nn(rows[...].astype(BF16), kt_mat[...]), shift)


def pack_rows(out_ref, flow, total, shift):
    n = flow.shape[1]
    out_ref[0:128, :] = flow.astype(BF16)
    high = total.astype(BF16).astype(F32)
    kind = lax.broadcasted_iota(jnp.int32, (16, n), 0)
    tail = jnp.where(kind == 0, high, jnp.where(kind == 1, total - high, jnp.where(kind == 2, shift, 0.0)))
    out_ref[128:144, :] = tail.astype(BF16)


def row_flow_kernel(parts, lb, kt_mat, base, b_t, held, own_out, other_out, pot_out, total_out, base_out, held_out,
                    rows, lhs, acc, sem):
    copy = pltpu.make_async_copy(held, held_out, sem)
    copy.start()
    core = lax.axis_index("core")
    level, total, shift, top = col_scales(parts, lb, rows)
    level_base = base[...] - top
    base_out[...] = level_base
    pot_out[...] = (level + level_base[0:1, :]) * (1.0 / C2)
    total_out[...] = total
    scale = rows[0:1, :] + rows[1:2, :]
    lhs[0:128, :] = (b_t[...].astype(F32) * scale).astype(BF16)
    lhs[128:144, :] = rows[...].astype(BF16)
    acc[...] = nn(lhs[...], kt_mat[...])
    for half, out in ((core, own_out), (1 - core, other_out)):
        part = acc[:, pl.ds(pl.multiple_of(half * 512, 512), 512)]
        pack_rows(out, part[0:128, :], part[128:129, :] + part[129:130, :], shift)
    copy.wait()


def merge(parts):
    tails = [p[128:144, :].astype(F32) for p in parts]
    shifts = [t[2:3, :] for t in tails]
    top = functools.reduce(jnp.maximum, shifts)
    flows, totals = [], []
    for p, t, s in zip(parts, tails, shifts):
        half = jnp.exp2(0.5 * (s - top))
        flows.append(p[0:128, :].astype(F32) * half * half)
        totals.append((t[0:1, :] + t[1:2, :]) * half * half)
    return pair_sum(flows), pair_sum(totals), top


def merge_kernel(own, received, out):
    flow, total, top = merge([own, received])
    pack_rows(out, flow, total, top)


def final_a(p0, p1, p2, p3, at_own, la, base, flow_out, pot_out):
    flow, total, top = merge([p0, p2, p1, p3])
    flow_t = flow / total
    level = jnp.log2(total) + (top - TOP - 2.0 * C2)
    for r in range(4):
        here = slice(r * 128, (r + 1) * 128)
        flow_out[here, :] = (flow_t[:, here] - at_own[:, here].astype(F32)).T
        pot_out[r : r + 1, :] = (la[r : r + 1, :] * LOG2E - level[:, here] - base[0:1, :]) * (1.0 / C2)


def final_kernel(p0, p1, p2, p3, at_own, la, base, sums, parts, total, b_t, own_pot, other_pot,
                 flow_a, pot_a, flow_b, pot_b):
    final_a(p0, p1, p2, p3, at_own, la, base, flow_a, pot_a)
    final_b(sums, parts, total, b_t, own_pot, other_pot, flow_b, pot_b)


def final_b(sums, parts, total, b_t, own_pot, other_pot, flow_out, pot_out):
    core = lax.axis_index("core")
    chunk = lax.axis_index("zy")
    shifts = [parts[d, 32:40, :] for d in range(NZY)]
    top = functools.reduce(jnp.maximum, shifts)
    acc = 0.0
    for d in range(NZY):
        half = jnp.exp2(0.5 * (shifts[d][0:1, 0:1] - top[0:1, 0:1]))
        acc = acc + sums[d].astype(F32) * half * half
    at = pl.multiple_of(chunk * CH, CH)
    unit = b_t[:, pl.ds(at, CH)].astype(F32)
    for r in range(2):
        here = slice(r * 128, (r + 1) * 128)
        denom = total[pl.ds(chunk * 2 + r, 1), :]
        flow_out[here, :] = (acc[:, here] / denom - unit[:, here]).T
    for k in range(NK):
        mine = own_pot[2 * k : 2 * k + 2, :]
        theirs = other_pot[2 * k : 2 * k + 2, :]
        pot_out[4 * k : 4 * k + 2, :] = jnp.where(core == 0, mine, theirs)
        pot_out[4 * k + 2 : 4 * k + 4, :] = jnp.where(core == 0, theirs, mine)


def sds(*shape, dtype=F32):
    return jax.ShapeDtypeStruct(shape, dtype)


VM = pl.BlockSpec(memory_space=pltpu.VMEM)
HB = pl.BlockSpec(memory_space=pltpu.HBM)


def call(kernel, ins, outs, scratch=(), flops=0, bytes_accessed=0, trans=0, outside=()):
    return pl.pallas_call(
        kernel,
        in_specs=ins,
        out_specs=[HB if i in outside else VM for i in range(len(outs))],
        out_shape=outs,
        scratch_shapes=list(scratch),
        compiler_params=pltpu.CompilerParams(vmem_limit_bytes=16 * 1024 * 1024),
        cost_estimate=pl.CostEstimate(flops=flops, bytes_accessed=bytes_accessed, transcendentals=trans),
    )


PASS = NR * NC


def on_device(desc_a, desc_b, logmass_a, logmass_b, g_start):
    swap = [(0, 1), (1, 0)]
    ring = [[(i, (i + s) % 4) for i in range(4)] for s in range(4)]
    keep = lambda x: pltpu.with_memory_space_constraint(x, pltpu.VMEM)
    stay = lambda x: pltpu.with_memory_space_constraint(x, pltpu.HBM)
    other_a = lax.ppermute(desc_a, "core", swap)

    b_t, at_own, right_own, scales, shift, lb, la_own = call(
        prep_kernel,
        [HB] * 5,
        [
            sds(DIM, NC, dtype=BF16),
            sds(DIM, 512, dtype=BF16),
            sds(2 * DIM, 512, dtype=BF16),
            sds(NC, 128),
            sds(8, 128),
            sds(32, 128),
            sds(4, 128),
        ],
        [
            pltpu.VMEM((NK, CH, DIM), BF16),
            pltpu.VMEM((512, DIM), BF16),
            pltpu.VMEM((64, 128), F32),
            pltpu.VMEM((64, 128), F32),
            pltpu.VMEM((32, 128), F32),
            pltpu.SemaphoreType.DMA((5,)),
        ],
        flops=8 * NC * DIM,
        bytes_accessed=2 * NC * DIM,
    )(
        stay(desc_b.reshape(NK, 2, CH, DIM)),
        stay(g_start.reshape(64, 128)),
        stay(logmass_b.reshape(64, 128)),
        stay(desc_a),
        stay(logmass_a.reshape(4, 128)),
    )

    kt_mat, a_t, msg = call(
        first_kernel,
        [VM] * 7,
        [pltpu.VMEM((NC, NR), BF16), sds(DIM, NR, dtype=BF16), sds(24, 128)],
        [pltpu.VMEM((2 * DIM, NR), BF16)],
        flops=2 * PASS * DIM,
        trans=PASS,
    )(at_own, right_own, other_a, la_own, b_t, scales, shift)

    def over_x(pair):
        return [pair] + [lax.ppermute(pair, "x", ring[s]) for s in (1, 2, 3)]

    pair, la = call(first_pair_kernel, [VM] * 2, [sds(16, 128), sds(8, 128)])(msg, lax.ppermute(msg, "core", swap))
    k_mat = call(
        kernel_matrix, [VM] * 2, [pltpu.VMEM((NR, NC), BF16)], flops=2 * PASS * DIM, trans=PASS
    )(a_t, b_t)[0]
    msg, base = call(
        col_kernel,
        [VM] * 6,
        [sds(NZY, 40, 128), sds(8, 128)],
        [pltpu.VMEM((16, NR), F32)],
        flops=2 * PASS * 16,
    )(*over_x(pair), la, keep(k_mat))

    parts = lax.all_to_all(msg, "zy", 0, 0)
    msg, base = call(
        row_kernel,
        [VM] * 4,
        [sds(16, 128), sds(8, 128)],
        [pltpu.VMEM((16, NC), F32)],
        flops=2 * PASS * 16,
    )(parts, lb, keep(kt_mat), base)

    pair = call(pair_kernel, [VM] * 2, [sds(16, 128)])(msg, lax.ppermute(msg, "core", swap))[0]
    msg, sums, base = call(
        last_col_kernel,
        [VM] * 8,
        [sds(NZY, 40, 128), pltpu.VMEM((NZY, DIM, CH), BF16), sds(8, 128)],
        [pltpu.VMEM((16, NR), F32), pltpu.VMEM((144, NR), BF16)],
        flops=2 * PASS * 144,
    )(*over_x(pair), la, keep(k_mat), base, a_t)
    parts = lax.all_to_all(msg, "zy", 0, 0)
    own, other, own_pot, total, base, sums = call(
        row_flow_kernel,
        [VM] * 6,
        [
            sds(144, 512, dtype=BF16),
            sds(144, 512, dtype=BF16),
            sds(32, 128),
            sds(32, 128),
            sds(8, 128),
            pltpu.HBM((NZY, DIM, CH), BF16),
        ],
        [pltpu.VMEM((16, NC), F32), pltpu.VMEM((144, NC), BF16), pltpu.VMEM((144, NR), F32), pltpu.SemaphoreType.DMA],
        flops=2 * PASS * 144,
        outside=(5,),
    )(parts, lb, keep(kt_mat), base, b_t, keep(sums))

    received = lax.ppermute(other, "core", swap)
    sums = lax.all_to_all(sums, "zy", 0, 0)
    other_pot = lax.ppermute(own_pot, "core", swap)
    mine = call(merge_kernel, [VM] * 2, [sds(144, 512, dtype=BF16)])(own, received)[0]
    others = over_x(mine)[1:]
    flow_a, pot_a, flow_b, pot_b = call(
        final_kernel, [VM] * 13, [sds(512, DIM), sds(4, 128), sds(CH, DIM), sds(64, 128)]
    )(mine, *others, at_own, la_own, base, sums, parts, total, b_t, own_pot, other_pot)
    return (pot_a.reshape(512), pot_b.reshape(8192), flow_a, flow_b)


def solution(mesh):
    fine = Mesh(mesh.devices.reshape(NZY, 2, 4), ("zy", "core", "x"))
    wide = ("zy", "core")
    return jax.shard_map(
        on_device,
        mesh=fine,
        in_specs=(P(wide, None), P("x", None), P(wide), P("x"), P("x")),
        out_specs=(P(wide), P("x"), P(wide, None), P(("x", "zy", "core"), None)),
        check_vma=False,
    )
```
